256 devices in a mesh: ha: 16 (over x, z_lo), wa: 16 (over z_hi, y, core).
Axes of the slice: x: 4, y: 4, z: 8 (z_hi: 2, z_lo: 4; z = z_hi * 4 + z_lo), core: 2. Of those that a mesh axis runs over, the one named last changes fastest.
Arguments:
- features: bfloat16 [4, 128, 512, 256], P(None, 'ha', 'wa'), may hold values from -6 to 6
- weights: bfloat16 [3, 3, 3, 256, 256], replicated, may hold values from -0.078125 to 0.078125
- cotangent: bfloat16 [4, 128, 512, 256], P(None, 'ha', 'wa'), may hold values from -6 to 6
Outputs:
- block_out: bfloat16 [4, 128, 512, 256], P(None, 'ha', 'wa')
- feature_grad: bfloat16 [4, 128, 512, 256], P(None, 'ha', 'wa')
- weight_grad: float32 [27, 256, 256], P(None, 'ha', 'wa')
The draws below stay inside these ranges and needn't reach their ends.
All inputs are finite; a program needn't handle non-finite values.
Results may differ from the reference program's by a relative error of at most 0.0032.
Values may be sent and summed in bfloat16 or wider, within the bound.
A program may use at most 256 MiB of HBM per device.

```python
import jax
import jax.numpy as jnp

C = 256
FRAMES = 4
NH = 128
NW = 512


def level_of(own_key, extent, cuts, smallest, top_value):
    def one(dim, blocks):
        steps = jax.random.uniform(jax.random.fold_in(jax.random.fold_in(own_key, 6), dim), (blocks,), jnp.float32, smallest / len(cuts), top_value / len(cuts))
        return jnp.repeat(jnp.exp(steps), extent[dim] // blocks).reshape((-1,) + (1,) * (len(extent) - dim - 1))

    loudness = one(*cuts[0])
    for cut in cuts[1:]:
        loudness = loudness * one(*cut)
    return loudness


def centred(stream_key, extent, scale, reach, cuts=(), dtype=jnp.bfloat16):
    gain = level_of(stream_key, extent, cuts, -0.22, 0.18) if cuts else 1.0
    entries = jax.random.normal(stream_key, extent, jnp.float32) * scale * gain
    return jnp.minimum(jnp.maximum(entries, -reach), reach).astype(dtype)


def setup_inputs(seed: int = 0) -> dict:
    key_list = jax.random.split(jax.random.key(seed), 4)
    features = centred(key_list[0], (FRAMES, NH, NW, C), 1.0, 6.0, ((1, 16), (2, 16)))
    weights = centred(key_list[1], (3, 3, 3, C, C), (27 * C) ** -0.5, 0.078125)
    cotangent = centred(key_list[2], (FRAMES, NH, NW, C), 1.0, 6.0, ((1, 16), (2, 16)))
    return dict(features=features, weights=weights, cotangent=cotangent)


def tap_conv(padded, kernel, frames, tile_rows, tile_cols):
    channels_in = padded.shape[3]
    running = jnp.zeros((frames * tile_rows * tile_cols, kernel.shape[4]), jnp.float32)
    for depth_tap in range(3):
        for row_tap in range(3):
            for col_tap in range(3):
                window = padded[depth_tap:depth_tap + frames, row_tap:row_tap + tile_rows, col_tap:col_tap + tile_cols].reshape(-1, channels_in)
                running = running + jnp.dot(window.astype(jnp.float32), kernel[depth_tap, row_tap, col_tap].astype(jnp.float32))
    return running

def reference(features, weights, cotangent):
    frames, height, breadth, channels = features.shape
    spatial = jnp.pad(features, ((0, 0), (1, 1), (1, 1), (0, 0)))
    padded = jnp.concatenate([spatial[:1], spatial[:1], spatial], axis=0)
    pre_act = tap_conv(padded, weights, frames, height, breadth).reshape(features.shape)
    logistic = jax.nn.sigmoid(pre_act)
    block_out = (features.astype(jnp.float32) + pre_act * logistic).astype(jnp.bfloat16)
    act_grad = (cotangent.astype(jnp.float32) * logistic * (1.0 + pre_act * (1.0 - logistic))).astype(jnp.bfloat16)
    grad_pad = jnp.pad(act_grad, ((2, 2), (1, 1), (1, 1), (0, 0)))
    flipped = jnp.swapaxes(jnp.flip(weights, (0, 1, 2)), 3, 4)
    input_part = tap_conv(grad_pad, flipped, frames + 2, height, breadth).reshape(frames + 2, height, breadth, channels)
    through = input_part[2:].at[0].add(input_part[0] + input_part[1])
    feature_grad = (cotangent.astype(jnp.float32) + through).astype(jnp.bfloat16)
    grad_flat = act_grad.reshape(-1, channels).astype(jnp.float32)
    tap_terms = []
    for depth_tap in range(3):
        for row_tap in range(3):
            for col_tap in range(3):
                window = padded[depth_tap:depth_tap + frames, row_tap:row_tap + height, col_tap:col_tap + breadth].reshape(-1, channels)
                tap_terms.append(jnp.dot(window.astype(jnp.float32).T, grad_flat))
    factor = 1.0 / jnp.sqrt(jnp.float32(frames * height * breadth))
    weight_grad = jnp.stack(tap_terms) * factor
    return (block_out, feature_grad, weight_grad)
```

```python
import jax
import jax.numpy as jnp
from jax import lax
from jax.experimental import pallas as pl
from jax.experimental.pallas import tpu as pltpu
from jax.sharding import PartitionSpec as P

MESH = pl.DeviceIdType.MESH
BF, F32 = jnp.bfloat16, jnp.float32
PAIRS = 14
FOLD = (((0, 4),), ((0, 3), (1, 2)), ((0, 0), (1, 1), (2, 2)), ((1, 0), (2, 1), (3, 2)))


def mm(a, b):
    return jnp.dot(a, b, preferred_element_type=F32)


def nt(a, b):
    return lax.dot_general(a, b, (((1,), (1,)), ((), ())), preferred_element_type=F32)


def iota(shape, dim):
    return lax.broadcasted_iota(jnp.int32, shape, dim)


def kernel(
    feat_hbm, w_hbm, cot_hbm,
    bo_hbm, fg_hbm, wg_ref,
    w_ref, wsum, tile, gtile, xc, xc2, xg, cot, bo, fg, gt, gt2,
    cols, gcols, left, right, gleft, gright,
    part, partb, r1, s1, s1b, r2, s2, of, ob, r3,
    local_sem, hs, hr, ghs, ghr, xcs, xcr, gts, gtr, s1s, s1r, s2s, s2r, s3s, s3r,
):
    ha, wa = lax.axis_index("ha"), lax.axis_index("wa")
    x, zlo = ha // 4, ha % 4
    zhi, y, core = wa // 8, (wa // 2) % 4, wa % 2
    z = zhi * 4 + zlo

    def device(dx=0, dy=0, dz=0, dc=0):
        nx, ny, nz, nc = (x + dx) % 4, (y + dy) % 4, (z + dz) % 8, (core + dc) % 2
        return (nx * 4 + nz % 4, (nz // 4) * 8 + ny * 2 + nc)

    other = device(dc=1)
    north, south, west, east = ha > 0, ha < 15, wa > 0, wa < 15
    sides = (
        (north, -1, 0), (south, 1, 0), (west, 0, -1), (east, 0, 1),
        (north & west, -1, -1), (north & east, -1, 1), (south & west, 1, -1), (south & east, 1, 1),
    )

    loads = [
        pltpu.make_async_copy(feat_hbm, tile.at[:, 1:9, 16:48, :], local_sem.at[0]),
        pltpu.make_async_copy(w_hbm, w_ref, local_sem.at[1]),
        pltpu.make_async_copy(cot_hbm, cot, local_sem.at[2]),
    ]
    for copy in loads:
        copy.start()

    barrier = pltpu.get_barrier_semaphore()
    count = 14
    for present, dr, dc in sides:
        @pl.when(present)
        def _():
            pl.semaphore_signal(barrier, inc=1, device_id=(ha + dr, wa + dc), device_id_type=MESH)
        count = count + present.astype(jnp.int32)
    peers = [device(dy=d) for d in (1, 2, 3)] + [device(dx=d) for d in (1, 2, 3)]
    peers += [device(dz=d) for d in range(1, 8)] + [other]
    for peer in peers:
        pl.semaphore_signal(barrier, inc=1, device_id=peer, device_id_type=MESH)

    m, n = iota((128, 1024), 0), iota((128, 1024), 1)
    column = jnp.where(m < 64, 31, 0)
    mm_ = m % 64
    pick = jnp.where(mm_ < 32, mm_ * 32, jnp.where(mm_ < 48, (mm_ - 32) * 256, (mm_ - 48) * 256 + 224)) + column
    select = jnp.where(pick == n, 1.0, 0.0).astype(BF)
    m, n = iota((640, 64), 0), iota((640, 64), 1)
    group = m // 16
    frame, row = group // 10, group % 10
    pick = jnp.where(row == 0, 32 + frame, jnp.where(row == 9, 48 + frame, frame * 8 + row - 1))
    spread = jnp.where(pick == n, 1.0, 0.0).astype(BF)

    def halo_copies(padded, packed, lhs, rhs, send, recv):
        row_src = {-1: padded.at[:, 1, 16:48, :], 1: padded.at[:, 8, 16:48, :]}
        row_dst = {-1: padded.at[:, 9, 16:48, :], 1: padded.at[:, 0, 16:48, :]}
        copies = []
        for i, (present, dr, dc) in enumerate(sides):
            if dc == 0:
                src, dst = row_src[dr], row_dst[dr]
            else:
                base = 0 if dc == 1 else 64
                target = lhs if dc == 1 else rhs
                if dr == 0:
                    src, dst = packed.at[base:base + 32], target.at[0:32]
                elif dr == -1:
                    src, dst = packed.at[base + 32:base + 48], target.at[48:64]
                else:
                    src, dst = packed.at[base + 48:base + 64], target.at[32:48]
            back = {(-1, 0): 1, (1, 0): 0, (0, -1): 3, (0, 1): 2, (-1, -1): 7, (-1, 1): 6, (1, -1): 5, (1, 1): 4}[(dr, dc)]
            copies.append((present, pltpu.make_async_remote_copy(
                src_ref=src, dst_ref=dst, send_sem=send.at[i], recv_sem=recv.at[back],
                device_id=(ha + dr, wa + dc), device_id_type=MESH)))
        return copies

    def halo_landing(padded, lhs, rhs):
        return (
            padded.at[:, 0, 16:48, :], padded.at[:, 9, 16:48, :], lhs.at[0:32], rhs.at[0:32],
            lhs.at[32:48], rhs.at[32:48], lhs.at[48:64], rhs.at[48:64],
        )

    def halo_wait(padded, lhs, rhs, recv):
        for i, ((present, dr, dc), ref) in enumerate(zip(sides, halo_landing(padded, lhs, rhs))):
            @pl.when(present)
            def _():
                pltpu.make_async_copy(ref, ref, recv.at[i]).wait()

            @pl.when(jnp.logical_not(present))
            def _():
                ref[...] = jnp.zeros(ref.shape, BF)

    def shifted(padded, lhs, rhs, out):
        padded[:, :, 0:16, :] = mm(spread, lhs[...]).astype(BF).reshape(4, 10, 16, 256)
        padded[:, :, 48:64, :] = mm(spread, rhs[...]).astype(BF).reshape(4, 10, 16, 256)
        for t in range(4):
            for r in range(10):
                for c in range(3):
                    out[t, r * 32:r * 32 + 32, c * 256:c * 256 + 256] = padded[t, r, 15 + c:47 + c, :]

    loads[0].wait()
    cols[...] = mm(select, tile[:, 1:9, 16:48, :].reshape(1024, 256)).astype(BF)
    pl.semaphore_wait(barrier, count)
    halo = halo_copies(tile, cols, left, right, hs, hr)
    for present, copy in halo:
        pl.when(present)(copy.start)
    loads[1].wait()
    for b in range(3):
        two = w_ref[b].astype(F32) + w_ref[3 + b].astype(F32)
        wsum[b] = two.astype(BF)
        wsum[3 + b] = (two + w_ref[6 + b].astype(F32)).astype(BF)
    loads[2].wait()
    halo_wait(tile, left, right, hr)
    shifted(tile, left, right, xc)
    xcopy = pltpu.make_async_remote_copy(
        src_ref=xc, dst_ref=xc2, send_sem=xcs, recv_sem=xcr, device_id=other, device_id_type=MESH)
    xcopy.start()

    gcopies = []
    for t in range(4):
        acc = None
        for f, a in FOLD[t]:
            for b in range(3):
                weight = w_ref[a * 3 + b] if a < 3 else wsum[(a - 3) * 3 + b]
                term = mm(xc[f, b * 32:b * 32 + 256, :], weight)
                acc = term if acc is None else acc + term
        logistic = jax.nn.sigmoid(acc)
        own = tile[t, 1:9, 16:48, :].reshape(256, 256).astype(F32)
        bo[t] = (own + acc * logistic).astype(BF).reshape(8, 32, 256)
        grad = cot[t].reshape(256, 256).astype(F32) * logistic * (1.0 + acc * (1.0 - logistic))
        grad = grad.astype(BF)
        gtile[t, 1:9, 16:48, :] = grad.reshape(8, 32, 256)
        gt[:, :, :, t * 256:t * 256 + 256] = grad.T.reshape(8, 2, 16, 256)
        copy = pltpu.make_async_remote_copy(
            src_ref=gt.at[:, 1 - core, :, t * 256:t * 256 + 256], dst_ref=gt2.at[:, :, t * 256:t * 256 + 256],
            send_sem=gts.at[t], recv_sem=gtr.at[t], device_id=other, device_id_type=MESH)
        copy.start()
        gcopies.append(copy)
    gcols[...] = mm(select, gtile[:, 1:9, 16:48, :].reshape(1024, 256)).astype(BF)
    ghalo = halo_copies(gtile, gcols, gleft, gright, ghs, ghr)
    for present, copy in ghalo:
        pl.when(present)(copy.start)
    bo_out = pltpu.make_async_copy(bo, bo_hbm, local_sem.at[0])
    bo_out.start()
    xcopy.wait_recv()
    for copy in gcopies:
        copy.wait_recv()

    low = iota((128, 128), 1) < 64

    def tap_term(tap):
        a, b, c = tap // 9, (tap // 3) % 3, tap % 3
        acc = None
        for lhs, rhs in ((gt, xc), (gt2, xc2)):
            for t in range(4):
                lanes = slice(t * 256, t * 256 + 256)
                one = gt[:, core, :, lanes] if lhs is gt else gt2[:, :, lanes]
                window = rhs[
                    jnp.maximum(t + a - 2, 0), pl.ds(pl.multiple_of(b * 32, 32), 256),
                    pl.ds(pl.multiple_of(c * 256, 256), 256)]
                term = mm(one.reshape(128, 256), window)
                acc = term if acc is None else acc + term
        return acc

    def tap_pair(p):
        first, second = tap_term(2 * p), tap_term(jnp.minimum(2 * p + 1, 26))
        for half in range(2):
            lanes = slice(half * 128, half * 128 + 128)
            one, two = first[:, lanes], second[:, lanes]
            both = (jnp.where(low, one, pltpu.roll(two, 64, 1)), jnp.where(low, pltpu.roll(one, 64, 1), two))
            for k, block in enumerate(both):
                for zz in range(2):
                    for yy in range(4):
                        rows = block[(zz * 4 + yy) * 16:(zz * 4 + yy) * 16 + 16]
                        part[p, yy, 2 * half + k, zz * 16:zz * 16 + 16] = rows
                        partb[p, yy, 2 * half + k, zz * 16:zz * 16 + 16] = rows.astype(BF)

    def first_copy(p, d, by_y):
        source = partb.at[p, (y + d) % 4] if by_y else partb.at[p, :, (x + d) % 4]
        return pltpu.make_async_remote_copy(
            src_ref=source, dst_ref=r1.at[p, d - 1], send_sem=s1s.at[p, d - 1], recv_sem=s1r.at[p, d - 1],
            device_id=device(dy=d) if by_y else device(dx=d), device_id_type=MESH)

    def second_copy(p, d, by_y):
        source = s1b.at[p, (y + d) % 4] if by_y else s1b.at[p, (x + d) % 4]
        return pltpu.make_async_remote_copy(
            src_ref=source, dst_ref=r2.at[p, d - 1], send_sem=s2s.at[p, d - 1], recv_sem=s2r.at[p, d - 1],
            device_id=device(dy=d) if by_y else device(dx=d), device_id_type=MESH)

    @pl.loop(0, PAIRS // 2)
    def _(i):
        for k in range(2):
            p = 2 * i + k
            tap_pair(p)
            for d in (2, 1, 3):
                first_copy(p, d, k == 0).start()

    halo_wait(gtile, gleft, gright, ghr)
    shifted(gtile, gleft, gright, xg)
    for t in range(4):
        acc = cot[t].reshape(256, 256).astype(F32)
        terms = [(t + 2 - a, a) for a in range(3) if t + 2 - a < 4]
        if t == 0:
            terms = [(2, 0), (1, 3), (0, 4)]
        for f, a in terms:
            for b in range(3):
                for c in range(3):
                    index = a * 3 + 2 - b if a < 3 else (a - 3) * 3 + 2 - b
                    weight = (w_ref if a < 3 else wsum)[index, (2 - c) * 256:(2 - c) * 256 + 256, :]
                    acc = acc + nt(xg[f, b * 32:b * 32 + 256, c * 256:c * 256 + 256], weight)
        fg[t] = acc.astype(BF).reshape(8, 32, 256)
    fg_out = pltpu.make_async_copy(fg, fg_hbm, local_sem.at[1])
    fg_out.start()

    @pl.loop(0, PAIRS // 2)
    def _(i):
        for k in range(2):
            p = 2 * i + k
            for d in (1, 2, 3):
                first_copy(p, d, k == 0).wait_recv()
            total = part[p, y] if k == 0 else part[p, :, x]
            for d in range(3):
                total = total + r1[p, d].astype(F32)
            s1[p] = total
            s1b[p] = total.astype(BF)
            for d in (2, 1, 3):
                second_copy(p, d, k == 1).start()

    @pl.loop(0, PAIRS // 2)
    def _(i):
        for k in range(2):
            p = 2 * i + k
            for d in (1, 2, 3):
                second_copy(p, d, k == 1).wait_recv()
            total = s1[p, x] if k == 0 else s1[p, y]
            for d in range(3):
                total = total + r2[p, d].astype(F32)
            s2[p] = total
    s2[PAIRS] = jnp.zeros((32, 128), F32)
    s2[PAIRS + 1] = jnp.zeros((32, 128), F32)

    lane = iota((32, 128), 1)

    def exchange(one, two, width):
        lower = (lane // width) % 2 == 0
        return (jnp.where(lower, one, pltpu.roll(two, width, 1)),
                jnp.where(lower, pltpu.roll(one, 128 - width, 1), two))

    for q in range(4):
        v = [s2[4 * q + i] for i in range(4)]
        v[0], v[1] = exchange(v[0], v[1], 16)
        v[2], v[3] = exchange(v[2], v[3], 16)
        v[0], v[2] = exchange(v[0], v[2], 32)
        v[1], v[3] = exchange(v[1], v[3], 32)
        for i in range(4):
            for zz in range(2):
                of[i, zz, q] = v[i][zz * 16:zz * 16 + 16]
                ob[i, zz, q] = v[i][zz * 16:zz * 16 + 16].astype(BF)
    third = []
    for d in (4, 3, 5, 2, 6, 1, 7):
        nz = (z + d) % 8
        copy = pltpu.make_async_remote_copy(
            src_ref=ob.at[nz % 4, nz // 4], dst_ref=r3.at[d - 1], send_sem=s3s.at[d - 1], recv_sem=s3r.at[d - 1],
            device_id=device(dz=d), device_id_type=MESH)
        copy.start()
        third.append(copy)
    for copy in third:
        copy.wait_recv()
    total = of[zlo, zhi]
    for d in range(7):
        total = total + r3[d].astype(F32)
    wg_ref[...] = total * (1.0 / 512.0)

    for present, copy in halo + ghalo:
        pl.when(present)(copy.wait_send)
    xcopy.wait_send()
    for copy in gcopies:
        copy.wait_send()

    @pl.loop(0, PAIRS // 2)
    def _(i):
        for k in range(2):
            for d in (1, 2, 3):
                first_copy(2 * i + k, d, k == 0).wait_send()
                second_copy(2 * i + k, d, k == 1).wait_send()
    for copy in third:
        copy.wait_send()
    bo_out.wait()
    fg_out.wait()


def per_device(features, weights, cotangent):
    dma = pltpu.SemaphoreType.DMA
    anywhere = pl.BlockSpec(memory_space=pl.ANY)
    block = jax.ShapeDtypeStruct((4, 8, 32, 256), BF)
    block_out, feature_grad, packed = pl.pallas_call(
        kernel,
        out_shape=(block, block, jax.ShapeDtypeStruct((4, 16, 128), F32)),
        in_specs=[anywhere] * 3,
        out_specs=(anywhere, anywhere, pl.BlockSpec(memory_space=pltpu.VMEM)),
        scratch_shapes=[
            pltpu.VMEM((9, 768, 256), BF), pltpu.VMEM((6, 768, 256), BF),
            pltpu.VMEM((4, 10, 64, 256), BF), pltpu.VMEM((4, 10, 64, 256), BF),
            pltpu.VMEM((4, 320, 768), BF), pltpu.VMEM((4, 320, 768), BF), pltpu.VMEM((4, 320, 768), BF),
            pltpu.VMEM((4, 8, 32, 256), BF), pltpu.VMEM((4, 8, 32, 256), BF), pltpu.VMEM((4, 8, 32, 256), BF),
            pltpu.VMEM((8, 2, 16, 1024), BF), pltpu.VMEM((8, 16, 1024), BF),
            pltpu.VMEM((128, 256), BF), pltpu.VMEM((128, 256), BF),
            pltpu.VMEM((64, 256), BF), pltpu.VMEM((64, 256), BF), pltpu.VMEM((64, 256), BF), pltpu.VMEM((64, 256), BF),
            pltpu.VMEM((PAIRS, 4, 4, 32, 128), F32), pltpu.VMEM((PAIRS, 4, 4, 32, 128), BF),
            pltpu.VMEM((PAIRS, 3, 4, 32, 128), BF),
            pltpu.VMEM((PAIRS, 4, 32, 128), F32), pltpu.VMEM((PAIRS, 4, 32, 128), BF),
            pltpu.VMEM((PAIRS, 3, 32, 128), BF), pltpu.VMEM((PAIRS + 2, 32, 128), F32),
            pltpu.VMEM((4, 2, 4, 16, 128), F32), pltpu.VMEM((4, 2, 4, 16, 128), BF), pltpu.VMEM((7, 4, 16, 128), BF),
            dma((3,)), dma((8,)), dma((8,)), dma((8,)), dma((8,)), dma, dma, dma((4,)), dma((4,)),
            dma((PAIRS, 3)), dma((PAIRS, 3)), dma((PAIRS, 3)), dma((PAIRS, 3)), dma((7,)), dma((7,)),
        ],
        compiler_params=pltpu.CompilerParams(collective_id=0, has_side_effects=True, vmem_limit_bytes=60 << 20),
        cost_estimate=pl.CostEstimate(flops=9_000_000_000, bytes_accessed=6_000_000, transcendentals=300_000),
        name="conv_block",
    )(features, weights.reshape(9, 768, 256), cotangent)
    grads = packed.reshape(4, 16, 2, 4, 16).transpose(0, 3, 2, 4, 1).reshape(32, 16, 16)
    return block_out, feature_grad, grads[:27]


def solution(mesh):
    in_specs = (P(None, "ha", "wa", None), P(), P(None, "ha", "wa", None))
    out_specs = (P(None, "ha", "wa", None), P(None, "ha", "wa", None), P(None, "ha", "wa"))
    return jax.shard_map(
        per_device, mesh=mesh, in_specs=in_specs, out_specs=out_specs, check_vma=False
    )
```

```python
import jax
import jax.numpy as jnp
from jax import lax
from jax.experimental import pallas as pl
from jax.experimental.pallas import tpu as pltpu
from jax.sharding import PartitionSpec as P

MESH = pl.DeviceIdType.MESH
BF, F32 = jnp.bfloat16, jnp.float32
PAIRS = 14
FOLD = (((0, 4),), ((0, 3), (1, 2)), ((0, 0), (1, 1), (2, 2)), ((1, 0), (2, 1), (3, 2)))


def mm(a, b):
    return jnp.dot(a, b, preferred_element_type=F32)


def nt(a, b):
    return lax.dot_general(a, b, (((1,), (1,)), ((), ())), preferred_element_type=F32)


def iota(shape, dim):
    return lax.broadcasted_iota(jnp.int32, shape, dim)


def kernel(
    feat_hbm, w_hbm, cot_hbm,
    bo_hbm, fg_hbm, wg_ref,
    w_ref, wsum, tile, gtile, xc, xc2, xg, cot, bo, fg, acc_ref, fix_ref, hold, gt, gt2,
    cols, gcols, left, right, gleft, gright,
    part, partb, r1, s1, s1b, r2, s2, of, ob, r3,
    local_sem, hs, hr, ghs, ghr, xcs, xcr, gts, gtr, s1s, s1r, s2s, s2r, s3s, s3r,
):
    ha, wa = lax.axis_index("ha"), lax.axis_index("wa")
    x, zlo = ha // 4, ha % 4
    zhi, y, core = wa // 8, (wa // 2) % 4, wa % 2
    z = zhi * 4 + zlo

    def device(dx=0, dy=0, dz=0, dc=0):
        nx, ny, nz, nc = (x + dx) % 4, (y + dy) % 4, (z + dz) % 8, (core + dc) % 2
        return (nx * 4 + nz % 4, (nz // 4) * 8 + ny * 2 + nc)

    other = device(dc=1)
    north, south, west, east = ha > 0, ha < 15, wa > 0, wa < 15
    sides = (
        (north, -1, 0), (south, 1, 0), (west, 0, -1), (east, 0, 1),
        (north & west, -1, -1), (north & east, -1, 1), (south & west, 1, -1), (south & east, 1, 1),
    )

    loads = [
        pltpu.make_async_copy(feat_hbm, tile.at[:, 1:9, 16:48, :], local_sem.at[0]),
        pltpu.make_async_copy(w_hbm, w_ref, local_sem.at[1]),
        pltpu.make_async_copy(cot_hbm, cot, local_sem.at[2]),
    ]
    for copy in loads:
        copy.start()

    barrier = pltpu.get_barrier_semaphore()
    count = 14
    for present, dr, dc in sides:
        @pl.when(present)
        def _():
            pl.semaphore_signal(barrier, inc=1, device_id=(ha + dr, wa + dc), device_id_type=MESH)
        count = count + present.astype(jnp.int32)
    peers = [device(dy=d) for d in (1, 2, 3)] + [device(dx=d) for d in (1, 2, 3)]
    peers += [device(dz=d) for d in range(1, 8)] + [other]
    for peer in peers:
        pl.semaphore_signal(barrier, inc=1, device_id=peer, device_id_type=MESH)

    m, n = iota((128, 1024), 0), iota((128, 1024), 1)
    column = jnp.where(m < 64, 31, 0)
    place = m % 64
    pick = jnp.where(place < 32, place * 32, jnp.where(place < 48, (place - 32) * 256, (place - 48) * 256 + 224)) + column
    select = jnp.where(pick == n, 1.0, 0.0).astype(BF)
    m, n = iota((512, 32), 0), iota((512, 32), 1)
    spread = jnp.where(m // 16 == n, 1.0, 0.0).astype(BF)
    m, n = iota((128, 32), 0), iota((128, 32), 1)
    corner = jnp.where(m // 64 * 16 + (m % 64) // 16 == n, 1.0, 0.0).astype(BF)

    def halo_copies(padded, packed, lhs, rhs, send, recv):
        row_src = {-1: padded.at[:, 1, 16:48, :], 1: padded.at[:, 8, 16:48, :]}
        row_dst = {-1: padded.at[:, 9, 16:48, :], 1: padded.at[:, 0, 16:48, :]}
        copies = []
        for i, (present, dr, dc) in enumerate(sides):
            if dc == 0:
                src, dst = row_src[dr], row_dst[dr]
            else:
                base = 0 if dc == 1 else 64
                target = lhs if dc == 1 else rhs
                if dr == 0:
                    src, dst = packed.at[base:base + 32], target.at[0:32]
                elif dr == -1:
                    src, dst = packed.at[base + 32:base + 48], target.at[48:64]
                else:
                    src, dst = packed.at[base + 48:base + 64], target.at[32:48]
            back = {(-1, 0): 1, (1, 0): 0, (0, -1): 3, (0, 1): 2, (-1, -1): 7, (-1, 1): 6, (1, -1): 5, (1, 1): 4}[(dr, dc)]
            copies.append((present, pltpu.make_async_remote_copy(
                src_ref=src, dst_ref=dst, send_sem=send.at[i], recv_sem=recv.at[back],
                device_id=(ha + dr, wa + dc), device_id_type=MESH)))
        return copies

    def halo_wait(padded, lhs, rhs, recv, which):
        landing = (
            padded.at[:, 0, 16:48, :], padded.at[:, 9, 16:48, :], lhs.at[0:32], rhs.at[0:32],
            lhs.at[32:48], rhs.at[32:48], lhs.at[48:64], rhs.at[48:64],
        )
        for i in which:
            present, ref = sides[i][0], landing[i]

            @pl.when(present)
            def _():
                pltpu.make_async_copy(ref, ref, recv.at[i]).wait()

            @pl.when(jnp.logical_not(present))
            def _():
                ref[...] = jnp.zeros(ref.shape, BF)

    def shifted(padded, lhs, rhs, out, rows, centre):
        if 1 in rows:
            padded[:, 1:9, 0:16, :] = mm(spread, lhs[0:32]).astype(BF).reshape(4, 8, 16, 256)
            padded[:, 1:9, 48:64, :] = mm(spread, rhs[0:32]).astype(BF).reshape(4, 8, 16, 256)
        if 0 in rows:
            for side, lanes in ((lhs, slice(0, 16)), (rhs, slice(48, 64))):
                ends = mm(corner, side[32:64]).astype(BF).reshape(2, 4, 16, 256)
                padded[:, 0, lanes, :] = ends[0]
                padded[:, 9, lanes, :] = ends[1]
        for t in range(4):
            for r in rows:
                for c in range(3):
                    if c != 1 or centre:
                        out[c, t, r * 32:r * 32 + 32, :] = padded[t, r, 15 + c:47 + c, :]

    middle, ends = tuple(range(1, 9)), (0, 9)

    zero_rows = jnp.zeros((32, 256), BF)
    for c in range(3):
        for t in range(4):
            for r in ends:
                xc[c, t, r * 32:r * 32 + 32, :] = zero_rows
    loads[0].wait()
    cols[...] = mm(select, tile[:, 1:9, 16:48, :].reshape(1024, 256)).astype(BF)
    pl.semaphore_wait(barrier, count)
    halo = halo_copies(tile, cols, left, right, hs, hr)
    for i in (2, 3, 0, 1, 4, 5, 6, 7):
        pl.when(halo[i][0])(halo[i][1].start)
    for t in range(4):
        for r in middle:
            xc[1, t, r * 32:r * 32 + 32, :] = tile[t, r, 16:48, :]

    def x_copy(i):
        ref = (lambda b: (b.at[1, :, 32:288], b.at[0, :, 32:288], b.at[2, :, 32:288], b.at[:, :, 0:32], b.at[:, :, 288:320])[i])
        return pltpu.make_async_remote_copy(
            src_ref=ref(xc), dst_ref=ref(xc2), send_sem=xcs.at[i], recv_sem=xcr.at[i], device_id=other, device_id_type=MESH)

    x_copy(0).start()
    loads[1].wait()

    def forward(t, columns):
        total = None
        for f, a in FOLD[t]:
            for b in range(3):
                for c in columns:
                    lanes = slice(c * 256, c * 256 + 256)
                    weight = w_ref[a * 3 + b, lanes] if a < 3 else wsum[(a - 3) * 3 + b, lanes]
                    term = mm(xc[c, f, b * 32:b * 32 + 256, :], weight)
                    total = term if total is None else total + term
        return total

    for t in (3, 2):
        acc_ref[t] = forward(t, (1,))
    for b in range(3):
        two = w_ref[b].astype(F32) + w_ref[3 + b].astype(F32)
        wsum[b] = two.astype(BF)
        wsum[3 + b] = (two + w_ref[6 + b].astype(F32)).astype(BF)
    for t in (1, 0):
        acc_ref[t] = forward(t, (1,))
    halo_wait(tile, left, right, hr, (2, 3))
    shifted(tile, left, right, xc, middle, False)
    x_copy(1).start()
    x_copy(2).start()
    for t in range(4):
        acc_ref[t] += forward(t, (0, 2))
    halo_wait(tile, left, right, hr, (0, 1, 4, 5, 6, 7))
    shifted(tile, left, right, xc, ends, True)
    x_copy(3).start()
    x_copy(4).start()
    for side, (lo, b) in enumerate(((0, 0), (288, 2))):
        total = None
        for a in range(3):
            for c in range(3):
                rows = jnp.concatenate([xc[c, max(t + a - 2, 0), lo:lo + 32, :] for t in range(4)], axis=0)
                term = mm(rows, w_ref[a * 3 + b, c * 256:c * 256 + 256])
                total = term if total is None else total + term
        fix_ref[side] = total
    loads[2].wait()

    def g_copy(t):
        return pltpu.make_async_remote_copy(
            src_ref=gt.at[:, 1 - core, :, t * 256:t * 256 + 256], dst_ref=gt2.at[:, :, t * 256:t * 256 + 256],
            send_sem=gts.at[t], recv_sem=gtr.at[t], device_id=other, device_id_type=MESH)

    for t in range(4):
        acc_ref[t, 0:32] += fix_ref[0, t * 32:t * 32 + 32]
        acc_ref[t, 224:256] += fix_ref[1, t * 32:t * 32 + 32]
        acc = acc_ref[t]
        logistic = jax.nn.sigmoid(acc)
        own = tile[t, 1:9, 16:48, :].reshape(256, 256).astype(F32)
        bo[t] = (own + acc * logistic).astype(BF).reshape(8, 32, 256)
        grad = cot[t].reshape(256, 256).astype(F32) * logistic * (1.0 + acc * (1.0 - logistic))
        grad = grad.astype(BF)
        gtile[t, 1:9, 16:48, :] = grad.reshape(8, 32, 256)
        gt[:, :, :, t * 256:t * 256 + 256] = grad.T.reshape(8, 2, 16, 256)
        g_copy(t).start()

    low = iota((128, 128), 1) < 64

    def tap_term(tap, both):
        a, b, c = tap // 9, (tap // 3) % 3, tap % 3
        total = None
        for mine in both:
            for t in range(4):
                lanes = slice(t * 256, t * 256 + 256)
                one = gt[:, core, :, lanes] if mine else gt2[:, :, lanes]
                window = (xc if mine else xc2)[c, max(t + a - 2, 0), b * 32:b * 32 + 256, :]
                term = mm(one.reshape(128, 256), window)
                total = term if total is None else total + term
        return total

    def store_pair(p, by_y):
        for half in range(2):
            lanes = slice(half * 128, half * 128 + 128)
            one, two = hold[p % 4, 0, :, lanes], hold[p % 4, 1, :, lanes]
            both = (jnp.where(low, one, pltpu.roll(two, 64, 1)), jnp.where(low, pltpu.roll(one, 64, 1), two))
            for k, block in enumerate(both):
                for zz in range(2):
                    for yy in range(4):
                        rows = block[(zz * 4 + yy) * 16:(zz * 4 + yy) * 16 + 16]
                        i, j = (yy, 2 * half + k) if by_y else (2 * half + k, yy)
                        part[p, i, j, zz * 16:zz * 16 + 16] = rows
                        partb[p, i, j, zz * 16:zz * 16 + 16] = rows.astype(BF)

    def first_copy(p, d, by_y):
        return pltpu.make_async_remote_copy(
            src_ref=partb.at[p, ((y if by_y else x) + d) % 4], dst_ref=r1.at[p, d - 1],
            send_sem=s1s.at[p, d - 1], recv_sem=s1r.at[p, d - 1],
            device_id=device(dy=d) if by_y else device(dx=d), device_id_type=MESH)

    def second_copy(p, d, by_y):
        return pltpu.make_async_remote_copy(
            src_ref=s1b.at[p, ((y if by_y else x) + d) % 4], dst_ref=r2.at[p, d - 1],
            send_sem=s2s.at[p, d - 1], recv_sem=s2r.at[p, d - 1],
            device_id=device(dy=d) if by_y else device(dx=d), device_id_type=MESH)

    def third_copy(q, d):
        nz = (z + d) % 8
        return pltpu.make_async_remote_copy(
            src_ref=ob.at[nz % 4, nz // 4, q], dst_ref=r3.at[q, d - 1], send_sem=s3s.at[q, d - 1], recv_sem=s3r.at[q, d - 1],
            device_id=device(dz=d), device_id_type=MESH)

    def over_pairs(q, body):
        @pl.loop(2 * q, min(2 * q + 2, PAIRS // 2))
        def _(i):
            for k in range(2):
                body(2 * i + k, k == 0)

    def own_terms(pairs):
        for p in pairs:
            for i in range(2):
                hold[p, i] = tap_term(2 * p + i, (True,))

    def pair_terms(p):
        for i in range(2):
            tap = min(2 * p + i, 26)
            hold[p % 4, i] = hold[p, i] + tap_term(tap, (False,)) if p < 4 else tap_term(tap, (True, False))

    def weight_group(done, new):
        for p in new:
            pair_terms(p)
        for p in done:
            store_pair(p, p % 2 == 0)
        for p in done:
            for d in (2, 1, 3):
                first_copy(p, d, p % 2 == 0).start()

    def first_sum(q):
        def body(p, by_y):
            for d in (1, 2, 3):
                first_copy(p, d, by_y).wait_recv()
            total = part[p, y if by_y else x]
            for d in range(3):
                total = total + r1[p, d].astype(F32)
            s1[p] = total
            s1b[p] = total.astype(BF)
            for d in (2, 1, 3):
                second_copy(p, d, not by_y).start()
        over_pairs(q, body)

    lane = iota((32, 128), 1)

    def exchange(one, two, width):
        lower = (lane // width) % 2 == 0
        return (jnp.where(lower, one, pltpu.roll(two, width, 1)),
                jnp.where(lower, pltpu.roll(one, 128 - width, 1), two))

    def second_sum(q):
        def body(p, by_y):
            for d in (1, 2, 3):
                second_copy(p, d, not by_y).wait_recv()
            total = s1[p, x if by_y else y]
            for d in range(3):
                total = total + r2[p, d].astype(F32)
            s2[p] = total
        over_pairs(q, body)
        v = [s2[4 * q + i] if 4 * q + i < PAIRS else jnp.zeros((32, 128), F32) for i in range(4)]
        v[0], v[1] = exchange(v[0], v[1], 16)
        v[2], v[3] = exchange(v[2], v[3], 16)
        v[0], v[2] = exchange(v[0], v[2], 32)
        v[1], v[3] = exchange(v[1], v[3], 32)
        for i in range(4):
            for zz in range(2):
                of[i, zz, q] = v[i][zz * 16:zz * 16 + 16]
                ob[i, zz, q] = v[i][zz * 16:zz * 16 + 16].astype(BF)
        for d in (4, 3, 5, 2, 6, 1, 7):
            third_copy(q, d).start()

    def feature_gradient(frames):
        jobs = {}
        for t in frames:
            terms = [(t + 2 - a, a) for a in range(3) if t + 2 - a < 4] if t else [(2, 0), (1, 3), (0, 4)]
            jobs[t] = [(f, a, b, c) for f, a in terms for b in range(3) for c in range(3)]
        totals = dict.fromkeys(frames)
        for i in range(max(len(job) for job in jobs.values())):
            for t in frames:
                if i < len(jobs[t]):
                    f, a, b, c = jobs[t][i]
                    index = a * 3 + 2 - b if a < 3 else (a - 3) * 3 + 2 - b
                    weight = (w_ref if a < 3 else wsum)[index, (2 - c) * 256:(2 - c) * 256 + 256, :]
                    term = nt(xg[c, f, b * 32:b * 32 + 256, :], weight)
                    totals[t] = term if totals[t] is None else totals[t] + term
        for t in frames:
            total = totals[t] + cot[t].reshape(256, 256).astype(F32)
            fg[t] = total.astype(BF).reshape(8, 32, 256)

    ghalo = halo_copies(gtile, gcols, gleft, gright, ghs, ghr)
    for i in (0, 1):
        pl.when(ghalo[i][0])(ghalo[i][1].start)
    own_terms(range(4))
    for t in range(4):
        g_copy(t).wait_recv()
    for i in range(5):
        x_copy(i).wait_recv()
    weight_group((), (0,))
    weight_group((0,), (1,))
    weight_group((1,), (2, 3))
    gcols[...] = mm(select, gtile[:, 1:9, 16:48, :].reshape(1024, 256)).astype(BF)
    for i in range(2, 8):
        pl.when(ghalo[i][0])(ghalo[i][1].start)
    weight_group((2, 3), (4, 5))
    weight_group((4, 5), (6, 7))
    weight_group((6, 7), (8, 9))
    weight_group((8, 9), (10, 11))
    bo_out = pltpu.make_async_copy(bo, bo_hbm, local_sem.at[0])
    bo_out.start()
    halo_wait(gtile, gleft, gright, ghr, range(8))
    shifted(gtile, gleft, gright, xg, tuple(range(10)), True)
    weight_group((10, 11), (12, 13))
    weight_group((12, 13), ())
    feature_gradient((3, 2))
    first_sum(0)
    first_sum(1)
    feature_gradient((1, 0))
    fg_out = pltpu.make_async_copy(fg, fg_hbm, local_sem.at[1])
    fg_out.start()
    second_sum(0)
    first_sum(2)
    second_sum(1)
    first_sum(3)
    second_sum(2)
    second_sum(3)
    for q in range(4):
        for d in range(1, 8):
            third_copy(q, d).wait_recv()
        total = of[zlo, zhi, q]
        for d in range(7):
            total = total + r3[q, d].astype(F32)
        wg_ref[q] = total * (1.0 / 512.0)

    for present, copy in halo + ghalo:
        pl.when(present)(copy.wait_send)
    for i in range(5):
        x_copy(i).wait_send()
    for t in range(4):
        g_copy(t).wait_send()

    @pl.loop(0, PAIRS // 2)
    def _(i):
        for k in range(2):
            for d in (1, 2, 3):
                first_copy(2 * i + k, d, k == 0).wait_send()
                second_copy(2 * i + k, d, k == 1).wait_send()

    @pl.loop(0, 4)
    def _(q):
        for d in range(1, 8):
            third_copy(q, d).wait_send()
    bo_out.wait()
    fg_out.wait()


def finish(bo_in, fg_in, packed, bo_out, fg_out, wg_out, flat, sems):
    copies = [pltpu.make_async_copy(bo_in, bo_out, sems.at[0]), pltpu.make_async_copy(fg_in, fg_out, sems.at[1])]
    for copy in copies:
        copy.start()
    for q in range(4):
        flipped = packed[q].T
        for e in range(8):
            tap = 8 * q + 2 * (e % 4) + e // 4
            flat[tap * 16:tap * 16 + 16, :] = flipped[e * 16:e * 16 + 16, :]
    for k in range(16):
        wg_out[k] = flat[pl.ds(k, 32, stride=16), :].T[:, :27]
    for copy in copies:
        copy.wait()


def per_device(features, weights, cotangent):
    dma = pltpu.SemaphoreType.DMA
    anywhere = pl.BlockSpec(memory_space=pl.ANY)
    vmem = pl.BlockSpec(memory_space=pltpu.VMEM)
    block = jax.ShapeDtypeStruct((4, 8, 32, 256), BF)
    block_out, feature_grad, packed = pl.pallas_call(
        kernel,
        out_shape=(block, block, jax.ShapeDtypeStruct((4, 16, 128), F32)),
        in_specs=[anywhere] * 3,
        out_specs=(anywhere, anywhere, vmem),
        scratch_shapes=[
            pltpu.VMEM((9, 768, 256), BF), pltpu.VMEM((6, 768, 256), BF),
            pltpu.VMEM((4, 10, 64, 256), BF), pltpu.VMEM((4, 10, 64, 256), BF),
            pltpu.VMEM((3, 4, 320, 256), BF), pltpu.VMEM((3, 4, 320, 256), BF), pltpu.VMEM((3, 4, 320, 256), BF),
            pltpu.VMEM((4, 8, 32, 256), BF), pltpu.VMEM((4, 8, 32, 256), BF), pltpu.VMEM((4, 8, 32, 256), BF),
            pltpu.VMEM((4, 256, 256), F32), pltpu.VMEM((2, 128, 256), F32), pltpu.VMEM((4, 2, 128, 256), F32),
            pltpu.VMEM((8, 2, 16, 1024), BF), pltpu.VMEM((8, 16, 1024), BF),
            pltpu.VMEM((128, 256), BF), pltpu.VMEM((128, 256), BF),
            pltpu.VMEM((64, 256), BF), pltpu.VMEM((64, 256), BF), pltpu.VMEM((64, 256), BF), pltpu.VMEM((64, 256), BF),
            pltpu.VMEM((PAIRS, 4, 4, 32, 128), F32), pltpu.VMEM((PAIRS, 4, 4, 32, 128), BF),
            pltpu.VMEM((PAIRS, 3, 4, 32, 128), BF),
            pltpu.VMEM((PAIRS, 4, 32, 128), F32), pltpu.VMEM((PAIRS, 4, 32, 128), BF),
            pltpu.VMEM((PAIRS, 3, 32, 128), BF), pltpu.VMEM((PAIRS, 32, 128), F32),
            pltpu.VMEM((4, 2, 4, 16, 128), F32), pltpu.VMEM((4, 2, 4, 16, 128), BF), pltpu.VMEM((4, 7, 16, 128), BF),
            dma((3,)), dma((8,)), dma((8,)), dma((8,)), dma((8,)), dma((5,)), dma((5,)), dma((4,)), dma((4,)),
            dma((PAIRS, 3)), dma((PAIRS, 3)), dma((PAIRS, 3)), dma((PAIRS, 3)), dma((4, 7)), dma((4, 7)),
        ],
        compiler_params=pltpu.CompilerParams(collective_id=0, has_side_effects=True, vmem_limit_bytes=60 << 20),
        cost_estimate=pl.CostEstimate(flops=9_000_000_000, bytes_accessed=6_000_000, transcendentals=300_000),
        name="conv_block",
    )(features, weights.reshape(9, 768, 256), cotangent)
    block_out, feature_grad, grads = pl.pallas_call(
        finish,
        out_shape=(block, block, jax.ShapeDtypeStruct((16, 16, 27), F32)),
        in_specs=[vmem] * 3,
        out_specs=(anywhere, anywhere, vmem),
        scratch_shapes=[pltpu.VMEM((512, 16), F32), dma((2,))],
        name="finish",
    )(block_out, feature_grad, packed)
    return block_out, feature_grad, grads.transpose(2, 0, 1)


def solution(mesh):
    in_specs = (P(None, "ha", "wa", None), P(), P(None, "ha", "wa", None))
    out_specs = (P(None, "ha", "wa", None), P(None, "ha", "wa", None), P(None, "ha", "wa"))
    return jax.shard_map(
        per_device, mesh=mesh, in_specs=in_specs, out_specs=out_specs, check_vma=False
    )
```

```python
import jax
import jax.numpy as jnp
from jax import lax
from jax.experimental import pallas as pl
from jax.experimental.pallas import tpu as pltpu
from jax.sharding import PartitionSpec as P

MESH = pl.DeviceIdType.MESH
BF, F32 = jnp.bfloat16, jnp.float32
PAIRS = 14
FOLD = (((0, 4),), ((0, 3), (1, 2)), ((0, 0), (1, 1), (2, 2)), ((1, 0), (2, 1), (3, 2)))


def mm(a, b):
    return jnp.dot(a, b, preferred_element_type=F32)


def nt(a, b):
    return lax.dot_general(a, b, (((1,), (1,)), ((), ())), preferred_element_type=F32)


def iota(shape, dim):
    return lax.broadcasted_iota(jnp.int32, shape, dim)


def kernel(
    feat_hbm, w_hbm, cot_hbm,
    bo_hbm, fg_hbm, wg_ref,
    w_ref, wsum, tile, gtile, xc, xc2, xg, cot, bo, fg, acc_ref, fix_ref, hold, gt, gt2,
    cols, gcols, left, right, gleft, gright,
    part, partb, r1, s1, s1b, r2, s2, of, ob, r3,
    local_sem, hs, hr, ghr, xcs, xcr, gts, gtr, s1s, s1r, s2s, s2r, s3s, s3r,
):
    ha, wa = lax.axis_index("ha"), lax.axis_index("wa")
    x, zlo = ha // 4, ha % 4
    zhi, y, core = wa // 8, (wa // 2) % 4, wa % 2
    z = zhi * 4 + zlo

    def device(dx=0, dy=0, dz=0, dc=0):
        nx, ny, nz, nc = (x + dx) % 4, (y + dy) % 4, (z + dz) % 8, (core + dc) % 2
        return (nx * 4 + nz % 4, (nz // 4) * 8 + ny * 2 + nc)

    other = device(dc=1)
    north, south, west, east = ha > 0, ha < 15, wa > 0, wa < 15
    sides = (
        (north, -1, 0), (south, 1, 0), (west, 0, -1), (east, 0, 1),
        (north & west, -1, -1), (north & east, -1, 1), (south & west, 1, -1), (south & east, 1, 1),
    )

    loads = [
        pltpu.make_async_copy(feat_hbm, tile.at[:, 1:9, 16:48, :], local_sem.at[0]),
        pltpu.make_async_copy(w_hbm, w_ref, local_sem.at[1]),
        pltpu.make_async_copy(cot_hbm, cot, local_sem.at[2]),
    ]
    for copy in loads:
        copy.start()

    barrier = pltpu.get_barrier_semaphore()
    count = 14
    for present, dr, dc in sides:
        @pl.when(present)
        def _():
            pl.semaphore_signal(barrier, inc=1, device_id=(ha + dr, wa + dc), device_id_type=MESH)
        count = count + present.astype(jnp.int32)
    peers = [device(dy=d) for d in (1, 2, 3)] + [device(dx=d) for d in (1, 2, 3)]
    peers += [device(dz=d) for d in range(1, 8)] + [other]
    for peer in peers:
        pl.semaphore_signal(barrier, inc=1, device_id=peer, device_id_type=MESH)

    m, n = iota((128, 1024), 0), iota((128, 1024), 1)
    column = jnp.where(m < 64, 31, 0)
    place = m % 64
    pick = jnp.where(place < 32, place * 32, jnp.where(place < 48, (place - 32) * 256, (place - 48) * 256 + 224)) + column
    select = jnp.where(pick == n, 1.0, 0.0).astype(BF)
    m, n = iota((512, 32), 0), iota((512, 32), 1)
    spread = jnp.where(m // 16 == n, 1.0, 0.0).astype(BF)
    m, n = iota((128, 32), 0), iota((128, 32), 1)
    corner = jnp.where(m // 64 * 16 + (m % 64) // 16 == n, 1.0, 0.0).astype(BF)

    def halo_copies(padded, packed, lhs, rhs, send, recv):
        row_src = {-1: padded.at[:, 1, 16:48, :], 1: padded.at[:, 8, 16:48, :]}
        row_dst = {-1: padded.at[:, 9, 16:48, :], 1: padded.at[:, 0, 16:48, :]}
        copies = []
        for i, (present, dr, dc) in enumerate(sides):
            if dc == 0:
                src, dst = row_src[dr], row_dst[dr]
            else:
                base = 0 if dc == 1 else 64
                target = lhs if dc == 1 else rhs
                if dr == 0:
                    src, dst = packed.at[base:base + 32], target.at[0:32]
                elif dr == -1:
                    src, dst = packed.at[base + 32:base + 48], target.at[48:64]
                else:
                    src, dst = packed.at[base + 48:base + 64], target.at[32:48]
            back = {(-1, 0): 1, (1, 0): 0, (0, -1): 3, (0, 1): 2, (-1, -1): 7, (-1, 1): 6, (1, -1): 5, (1, 1): 4}[(dr, dc)]
            copies.append((present, pltpu.make_async_remote_copy(
                src_ref=src, dst_ref=dst, send_sem=send.at[i], recv_sem=recv.at[back],
                device_id=(ha + dr, wa + dc), device_id_type=MESH)))
        return copies

    def halo_wait(padded, lhs, rhs, recv, which):
        landing = (
            padded.at[:, 0, 16:48, :], padded.at[:, 9, 16:48, :], lhs.at[0:32], rhs.at[0:32],
            lhs.at[32:48], rhs.at[32:48], lhs.at[48:64], rhs.at[48:64],
        )
        for i in which:
            present, ref = sides[i][0], landing[i]

            @pl.when(present)
            def _():
                pltpu.make_async_copy(ref, ref, recv.at[i]).wait()

            @pl.when(jnp.logical_not(present))
            def _():
                ref[...] = jnp.zeros(ref.shape, BF)

    def shifted(padded, lhs, rhs, out, rows, centre):
        if 1 in rows:
            padded[:, 1:9, 0:16, :] = mm(spread, lhs[0:32]).astype(BF).reshape(4, 8, 16, 256)
            padded[:, 1:9, 48:64, :] = mm(spread, rhs[0:32]).astype(BF).reshape(4, 8, 16, 256)
        if 0 in rows:
            for side, lanes in ((lhs, slice(0, 16)), (rhs, slice(48, 64))):
                ends = mm(corner, side[32:64]).astype(BF).reshape(2, 4, 16, 256)
                padded[:, 0, lanes, :] = ends[0]
                padded[:, 9, lanes, :] = ends[1]
        for t in range(4):
            for r in rows:
                for c in range(3):
                    if c != 1 or centre:
                        out[c, t, r * 32:r * 32 + 32, :] = padded[t, r, 15 + c:47 + c, :]

    middle, ends = tuple(range(1, 9)), (0, 9)

    zero_rows = jnp.zeros((32, 256), BF)
    for c in range(3):
        for t in range(4):
            for r in ends:
                xc[c, t, r * 32:r * 32 + 32, :] = zero_rows
    loads[0].wait()
    cols[...] = mm(select, tile[:, 1:9, 16:48, :].reshape(1024, 256)).astype(BF)
    pl.semaphore_wait(barrier, count)
    halo = halo_copies(tile, cols, left, right, hs, hr)
    for i in (2, 3, 0, 1, 4, 5, 6, 7):
        pl.when(halo[i][0])(halo[i][1].start)
    for t in range(4):
        for r in middle:
            xc[1, t, r * 32:r * 32 + 32, :] = tile[t, r, 16:48, :]

    def x_copy(i):
        ref = (lambda b: (b.at[1, :, 32:288], b.at[0, :, 32:288], b.at[2, :, 32:288], b.at[:, :, 0:32], b.at[:, :, 288:320])[i])
        return pltpu.make_async_remote_copy(
            src_ref=ref(xc), dst_ref=ref(xc2), send_sem=xcs, recv_sem=xcr, device_id=other, device_id_type=MESH)

    loads[1].wait()

    def forward(t, columns):
        total = None
        for f, a in FOLD[t]:
            for b in range(3):
                for c in columns:
                    lanes = slice(c * 256, c * 256 + 256)
                    weight = w_ref[a * 3 + b, lanes] if a < 3 else wsum[(a - 3) * 3 + b, lanes]
                    term = mm(xc[c, f, b * 32:b * 32 + 256, :], weight)
                    total = term if total is None else total + term
        return total

    for t in (3, 2):
        acc_ref[t] = forward(t, (1,))
    for b in range(3):
        two = w_ref[b].astype(F32) + w_ref[3 + b].astype(F32)
        wsum[b] = two.astype(BF)
        wsum[3 + b] = (two + w_ref[6 + b].astype(F32)).astype(BF)
    for t in (1, 0):
        acc_ref[t] = forward(t, (1,))
    halo_wait(tile, left, right, hr, (2, 3))
    shifted(tile, left, right, xc, middle, False)
    for i in range(3):
        x_copy(i).start()
    for t in range(4):
        acc_ref[t] += forward(t, (0, 2))
    halo_wait(tile, left, right, hr, (0, 1, 4, 5, 6, 7))
    shifted(tile, left, right, xc, ends, True)
    x_copy(3).start()
    x_copy(4).start()
    for side, (lo, b) in enumerate(((0, 0), (288, 2))):
        total = None
        for a in range(3):
            for c in range(3):
                rows = jnp.concatenate([xc[c, max(t + a - 2, 0), lo:lo + 32, :] for t in range(4)], axis=0)
                term = mm(rows, w_ref[a * 3 + b, c * 256:c * 256 + 256])
                total = term if total is None else total + term
        fix_ref[side] = total
    loads[2].wait()

    def g_copy(t):
        return pltpu.make_async_remote_copy(
            src_ref=gt.at[:, 1 - core, :, t * 256:t * 256 + 256], dst_ref=gt2.at[:, :, t * 256:t * 256 + 256],
            send_sem=gts, recv_sem=gtr, device_id=other, device_id_type=MESH)

    for t in range(4):
        acc_ref[t, 0:32] += fix_ref[0, t * 32:t * 32 + 32]
        acc_ref[t, 224:256] += fix_ref[1, t * 32:t * 32 + 32]
        acc = acc_ref[t]
        logistic = jax.nn.sigmoid(acc)
        own = tile[t, 1:9, 16:48, :].reshape(256, 256).astype(F32)
        bo[t] = (own + acc * logistic).astype(BF).reshape(8, 32, 256)
        grad = cot[t].reshape(256, 256).astype(F32) * logistic * (1.0 + acc * (1.0 - logistic))
        grad = grad.astype(BF)
        gtile[t, 1:9, 16:48, :] = grad.reshape(8, 32, 256)
        gt[:, :, :, t * 256:t * 256 + 256] = grad.T.reshape(8, 2, 16, 256)
        g_copy(t).start()

    low = iota((128, 128), 1) < 64

    def tap_term(tap, both):
        a, b, c = tap // 9, (tap // 3) % 3, tap % 3
        total = None
        for mine in both:
            for t in range(4):
                lanes = slice(t * 256, t * 256 + 256)
                one = gt[:, core, :, lanes] if mine else gt2[:, :, lanes]
                window = (xc if mine else xc2)[c, max(t + a - 2, 0), b * 32:b * 32 + 256, :]
                term = mm(one.reshape(128, 256), window)
                total = term if total is None else total + term
        return total

    def store_pair(p, by_y):
        for half in range(2):
            lanes = slice(half * 128, half * 128 + 128)
            one, two = hold[p % 4, 0, :, lanes], hold[p % 4, 1, :, lanes]
            both = (jnp.where(low, one, pltpu.roll(two, 64, 1)), jnp.where(low, pltpu.roll(one, 64, 1), two))
            for k, block in enumerate(both):
                for zz in range(2):
                    for yy in range(4):
                        rows = block[(zz * 4 + yy) * 16:(zz * 4 + yy) * 16 + 16]
                        i, j = (yy, 2 * half + k) if by_y else (2 * half + k, yy)
                        part[p, i, j, zz * 16:zz * 16 + 16] = rows
                        partb[p, i, j, zz * 16:zz * 16 + 16] = rows.astype(BF)

    def arrived(ref, sem):
        pltpu.make_async_copy(ref, ref, sem).wait()

    def first_copy(p, d, by_y):
        return pltpu.make_async_remote_copy(
            src_ref=partb.at[p, ((y if by_y else x) + d) % 4], dst_ref=r1.at[p, d - 1],
            send_sem=s1s, recv_sem=s1r.at[p // 4],
            device_id=device(dy=d) if by_y else device(dx=d), device_id_type=MESH)

    def second_copy(p, d, by_y, q):
        return pltpu.make_async_remote_copy(
            src_ref=s1b.at[p, ((y if by_y else x) + d) % 4], dst_ref=r2.at[p, d - 1],
            send_sem=s2s, recv_sem=s2r.at[q],
            device_id=device(dy=d) if by_y else device(dx=d), device_id_type=MESH)

    def third_copy(q, d):
        nz = (z + d) % 8
        return pltpu.make_async_remote_copy(
            src_ref=ob.at[nz % 4, nz // 4, q], dst_ref=r3.at[q, d - 1], send_sem=s3s, recv_sem=s3r.at[q],
            device_id=device(dz=d), device_id_type=MESH)

    def over_pairs(q, body):
        @pl.loop(2 * q, min(2 * q + 2, PAIRS // 2))
        def _(i):
            for k in range(2):
                body(2 * i + k, k == 0)

    def own_terms(pairs):
        for p in pairs:
            for i in range(2):
                hold[p, i] = tap_term(2 * p + i, (True,))

    def pair_terms(p):
        for i in range(2):
            tap = min(2 * p + i, 26)
            hold[p % 4, i] = hold[p, i] + tap_term(tap, (False,)) if p < 4 else tap_term(tap, (True, False))

    def weight_group(done, new):
        for p in new:
            pair_terms(p)
        for p in done:
            store_pair(p, p % 2 == 0)
        for p in done:
            for d in (1, 3, 2):
                first_copy(p, d, p % 2 == 0).start()

    def first_sum(q):
        def body(p, by_y):
            total = part[p, y if by_y else x]
            for d in range(3):
                total = total + r1[p, d].astype(F32)
            s1[p] = total
            s1b[p] = total.astype(BF)
            for d in (1, 3, 2):
                second_copy(p, d, not by_y, q).start()
        arrived(r1.at[4 * q:min(4 * q + 4, PAIRS)], s1r.at[q])
        over_pairs(q, body)

    lane = iota((32, 128), 1)

    def exchange(one, two, width):
        lower = (lane // width) % 2 == 0
        return (jnp.where(lower, one, pltpu.roll(two, width, 1)),
                jnp.where(lower, pltpu.roll(one, 128 - width, 1), two))

    def second_sum(q):
        def body(p, by_y):
            total = s1[p, x if by_y else y]
            for d in range(3):
                total = total + r2[p, d].astype(F32)
            s2[p] = total
        arrived(r2.at[4 * q:min(4 * q + 4, PAIRS)], s2r.at[q])
        over_pairs(q, body)
        v = [s2[4 * q + i] if 4 * q + i < PAIRS else jnp.zeros((32, 128), F32) for i in range(4)]
        v[0], v[1] = exchange(v[0], v[1], 16)
        v[2], v[3] = exchange(v[2], v[3], 16)
        v[0], v[2] = exchange(v[0], v[2], 32)
        v[1], v[3] = exchange(v[1], v[3], 32)
        for i in range(4):
            for zz in range(2):
                of[i, zz, q] = v[i][zz * 16:zz * 16 + 16]
                ob[i, zz, q] = v[i][zz * 16:zz * 16 + 16].astype(BF)
        for d in (4, 3, 5, 2, 6, 1, 7):
            third_copy(q, d).start()

    def feature_gradient(t):
        terms = [(t + 2 - a, a) for a in range(3) if t + 2 - a < 4] if t else [(2, 0), (1, 3), (0, 4)]
        total = None
        for f, a in terms:
            for b in range(3):
                for c in range(3):
                    index = a * 3 + 2 - b if a < 3 else (a - 3) * 3 + 2 - b
                    weight = (w_ref if a < 3 else wsum)[index, (2 - c) * 256:(2 - c) * 256 + 256, :]
                    term = nt(xg[c, f, b * 32:b * 32 + 256, :], weight)
                    total = term if total is None else total + term
        total = total + cot[t].reshape(256, 256).astype(F32)
        fg[t] = total.astype(BF).reshape(8, 32, 256)

    for present, copy in halo:
        pl.when(present)(copy.wait_send)
    ghalo = halo_copies(gtile, gcols, gleft, gright, hs, ghr)
    for i in (0, 1):
        pl.when(ghalo[i][0])(ghalo[i][1].start)
    own_terms(range(4))
    arrived(gt2, gtr)
    arrived(xc2, xcr)
    weight_group((), (0,))
    weight_group((0,), (1,))
    weight_group((1,), (2, 3))
    gcols[...] = mm(select, gtile[:, 1:9, 16:48, :].reshape(1024, 256)).astype(BF)
    for i in range(2, 8):
        pl.when(ghalo[i][0])(ghalo[i][1].start)
    weight_group((2, 3), (4, 5))
    weight_group((4, 5), (6, 7))
    weight_group((6, 7), (8, 9))
    weight_group((8, 9), (10, 11))
    bo_out = pltpu.make_async_copy(bo, bo_hbm, local_sem.at[0])
    bo_out.start()
    halo_wait(gtile, gleft, gright, ghr, range(8))
    shifted(gtile, gleft, gright, xg, tuple(range(10)), True)
    weight_group((10, 11), (12, 13))
    weight_group((12, 13), ())
    feature_gradient(3)
    feature_gradient(2)
    first_sum(0)
    first_sum(1)
    feature_gradient(1)
    feature_gradient(0)
    fg_out = pltpu.make_async_copy(fg, fg_hbm, local_sem.at[1])
    fg_out.start()
    second_sum(0)
    first_sum(2)
    second_sum(1)
    first_sum(3)
    second_sum(2)
    second_sum(3)
    for q in range(4):
        arrived(r3.at[q], s3r.at[q])
        total = of[zlo, zhi, q]
        for d in range(7):
            total = total + r3[q, d].astype(F32)
        wg_ref[q] = total * (1.0 / 512.0)

    for present, copy in ghalo:
        pl.when(present)(copy.wait_send)
    arrived(xc, xcs)
    arrived(gt2, gts)
    arrived(r1, s1s)
    arrived(r2, s2s)
    arrived(r3, s3s)
    bo_out.wait()
    fg_out.wait()


def finish(bo_in, fg_in, packed, bo_out, fg_out, wg_out, flat, sems):
    copies = [pltpu.make_async_copy(bo_in, bo_out, sems.at[0]), pltpu.make_async_copy(fg_in, fg_out, sems.at[1])]
    for copy in copies:
        copy.start()
    for q in range(4):
        flipped = packed[q].T
        for e in range(8):
            tap = 8 * q + 2 * (e % 4) + e // 4
            flat[tap * 16:tap * 16 + 16, :] = flipped[e * 16:e * 16 + 16, :]
    for k in range(16):
        wg_out[k] = flat[pl.ds(k, 32, stride=16), :].T[:, :27]
    for copy in copies:
        copy.wait()


def per_device(features, weights, cotangent):
    dma = pltpu.SemaphoreType.DMA
    anywhere = pl.BlockSpec(memory_space=pl.ANY)
    vmem = pl.BlockSpec(memory_space=pltpu.VMEM)
    block = jax.ShapeDtypeStruct((4, 8, 32, 256), BF)
    block_out, feature_grad, packed = pl.pallas_call(
        kernel,
        out_shape=(block, block, jax.ShapeDtypeStruct((4, 16, 128), F32)),
        in_specs=[anywhere] * 3,
        out_specs=(anywhere, anywhere, vmem),
        scratch_shapes=[
            pltpu.VMEM((9, 768, 256), BF), pltpu.VMEM((6, 768, 256), BF),
            pltpu.VMEM((4, 10, 64, 256), BF), pltpu.VMEM((4, 10, 64, 256), BF),
            pltpu.VMEM((3, 4, 320, 256), BF), pltpu.VMEM((3, 4, 320, 256), BF), pltpu.VMEM((3, 4, 320, 256), BF),
            pltpu.VMEM((4, 8, 32, 256), BF), pltpu.VMEM((4, 8, 32, 256), BF), pltpu.VMEM((4, 8, 32, 256), BF),
            pltpu.VMEM((4, 256, 256), F32), pltpu.VMEM((2, 128, 256), F32), pltpu.VMEM((4, 2, 128, 256), F32),
            pltpu.VMEM((8, 2, 16, 1024), BF), pltpu.VMEM((8, 16, 1024), BF),
            pltpu.VMEM((128, 256), BF), pltpu.VMEM((128, 256), BF),
            pltpu.VMEM((64, 256), BF), pltpu.VMEM((64, 256), BF), pltpu.VMEM((64, 256), BF), pltpu.VMEM((64, 256), BF),
            pltpu.VMEM((PAIRS, 4, 4, 32, 128), F32), pltpu.VMEM((PAIRS, 4, 4, 32, 128), BF),
            pltpu.VMEM((PAIRS, 3, 4, 32, 128), BF),
            pltpu.VMEM((PAIRS, 4, 32, 128), F32), pltpu.VMEM((PAIRS, 4, 32, 128), BF),
            pltpu.VMEM((PAIRS, 3, 32, 128), BF), pltpu.VMEM((PAIRS, 32, 128), F32),
            pltpu.VMEM((4, 2, 4, 16, 128), F32), pltpu.VMEM((4, 2, 4, 16, 128), BF), pltpu.VMEM((4, 7, 16, 128), BF),
            dma((3,)), dma((8,)), dma((8,)), dma((8,)), dma, dma, dma, dma,
            dma, dma((4,)), dma, dma((4,)), dma, dma((4,)),
        ],
        compiler_params=pltpu.CompilerParams(collective_id=0, has_side_effects=True, vmem_limit_bytes=60 << 20),
        cost_estimate=pl.CostEstimate(flops=9_000_000_000, bytes_accessed=6_000_000, transcendentals=300_000),
        name="conv_block",
    )(features, weights.reshape(9, 768, 256), cotangent)
    block_out, feature_grad, grads = pl.pallas_call(
        finish,
        out_shape=(block, block, jax.ShapeDtypeStruct((16, 16, 27), F32)),
        in_specs=[vmem] * 3,
        out_specs=(anywhere, anywhere, vmem),
        scratch_shapes=[pltpu.VMEM((512, 16), F32), dma((2,))],
        name="finish",
    )(block_out, feature_grad, packed)
    return block_out, feature_grad, grads.transpose(2, 0, 1)


def solution(mesh):
    in_specs = (P(None, "ha", "wa", None), P(), P(None, "ha", "wa", None))
    out_specs = (P(None, "ha", "wa", None), P(None, "ha", "wa", None), P(None, "ha", "wa"))
    return jax.shard_map(
        per_device, mesh=mesh, in_specs=in_specs, out_specs=out_specs, check_vma=False
    )
```

```python
import jax
import jax.numpy as jnp
from jax import lax
from jax.experimental import pallas as pl
from jax.experimental.pallas import tpu as pltpu
from jax.sharding import PartitionSpec as P

MESH = pl.DeviceIdType.MESH
BF, F32 = jnp.bfloat16, jnp.float32
PAIRS = 14
FOLD = (((0, 4),), ((0, 3), (1, 2)), ((0, 0), (1, 1), (2, 2)), ((1, 0), (2, 1), (3, 2)))


def mm(a, b):
    return jnp.dot(a, b, preferred_element_type=F32)


def nt(a, b):
    return lax.dot_general(a, b, (((1,), (1,)), ((), ())), preferred_element_type=F32)


def iota(shape, dim):
    return lax.broadcasted_iota(jnp.int32, shape, dim)


def kernel(
    feat_hbm, w_hbm, cot_hbm,
    bo_hbm, fg_hbm, wg_ref,
    w_ref, wsum, tile, gtile, xc, xc2, xg, cot, bo, fg, acc_ref, fix_ref, hold, gt, gt2,
    cols, gcols, left, right, gleft, gright,
    part, partb, r1, s1, s1b, r2, s2, of, ob, r3,
    local_sem, hs, hr, ghr, xcs, xcr, gts, gtr, s1s, s1r, s2s, s2r, s3s, s3r,
):
    ha, wa = lax.axis_index("ha"), lax.axis_index("wa")
    x, zlo = ha // 4, ha % 4
    zhi, y, core = wa // 8, (wa // 2) % 4, wa % 2
    z = zhi * 4 + zlo

    def device(dx=0, dy=0, dz=0, dc=0):
        nx, ny, nz, nc = (x + dx) % 4, (y + dy) % 4, (z + dz) % 8, (core + dc) % 2
        return (nx * 4 + nz % 4, (nz // 4) * 8 + ny * 2 + nc)

    other = device(dc=1)
    north, south, west, east = ha > 0, ha < 15, wa > 0, wa < 15
    sides = (
        (north, -1, 0), (south, 1, 0), (west, 0, -1), (east, 0, 1),
        (north & west, -1, -1), (north & east, -1, 1), (south & west, 1, -1), (south & east, 1, 1),
    )

    loads = [
        pltpu.make_async_copy(feat_hbm, tile.at[:, 1:9, 16:48, :], local_sem.at[0]),
        pltpu.make_async_copy(w_hbm, w_ref, local_sem.at[1]),
        pltpu.make_async_copy(cot_hbm, cot, local_sem.at[2]),
    ]
    for copy in loads:
        copy.start()

    barrier = pltpu.get_barrier_semaphore()
    count = 14
    for present, dr, dc in sides:
        @pl.when(present)
        def _():
            pl.semaphore_signal(barrier, inc=1, device_id=(ha + dr, wa + dc), device_id_type=MESH)
        count = count + present.astype(jnp.int32)
    peers = [device(dy=d) for d in (1, 2, 3)] + [device(dx=d) for d in (1, 2, 3)]
    peers += [device(dz=d) for d in range(1, 8)] + [other]
    for peer in peers:
        pl.semaphore_signal(barrier, inc=1, device_id=peer, device_id_type=MESH)

    m, n = iota((128, 1024), 0), iota((128, 1024), 1)
    column = jnp.where(m < 64, 31, 0)
    place = m % 64
    pick = jnp.where(place < 32, place * 32, jnp.where(place < 48, (place - 32) * 256, (place - 48) * 256 + 224)) + column
    select = jnp.where(pick == n, 1.0, 0.0).astype(BF)
    m, n = iota((512, 32), 0), iota((512, 32), 1)
    spread = jnp.where(m // 16 == n, 1.0, 0.0).astype(BF)
    m, n = iota((128, 32), 0), iota((128, 32), 1)
    corner = jnp.where(m // 64 * 16 + (m % 64) // 16 == n, 1.0, 0.0).astype(BF)

    def halo_copies(padded, packed, lhs, rhs, send, recv):
        row_src = {-1: padded.at[:, 1, 16:48, :], 1: padded.at[:, 8, 16:48, :]}
        row_dst = {-1: padded.at[:, 9, 16:48, :], 1: padded.at[:, 0, 16:48, :]}
        copies = []
        for i, (present, dr, dc) in enumerate(sides):
            if dc == 0:
                src, dst = row_src[dr], row_dst[dr]
            else:
                base = 0 if dc == 1 else 64
                target = lhs if dc == 1 else rhs
                if dr == 0:
                    src, dst = packed.at[base:base + 32], target.at[0:32]
                elif dr == -1:
                    src, dst = packed.at[base + 32:base + 48], target.at[48:64]
                else:
                    src, dst = packed.at[base + 48:base + 64], target.at[32:48]
            back = {(-1, 0): 1, (1, 0): 0, (0, -1): 3, (0, 1): 2, (-1, -1): 7, (-1, 1): 6, (1, -1): 5, (1, 1): 4}[(dr, dc)]
            copies.append((present, pltpu.make_async_remote_copy(
                src_ref=src, dst_ref=dst, send_sem=send.at[i], recv_sem=recv.at[back],
                device_id=(ha + dr, wa + dc), device_id_type=MESH)))
        return copies

    def halo_wait(padded, lhs, rhs, recv, which):
        landing = (
            padded.at[:, 0, 16:48, :], padded.at[:, 9, 16:48, :], lhs.at[0:32], rhs.at[0:32],
            lhs.at[32:48], rhs.at[32:48], lhs.at[48:64], rhs.at[48:64],
        )
        for i in which:
            present, ref = sides[i][0], landing[i]

            @pl.when(present)
            def _():
                pltpu.make_async_copy(ref, ref, recv.at[i]).wait()

            @pl.when(jnp.logical_not(present))
            def _():
                ref[...] = jnp.zeros(ref.shape, BF)

    def shifted(padded, lhs, rhs, out, rows, centre):
        if 1 in rows:
            padded[:, 1:9, 0:16, :] = mm(spread, lhs[0:32]).astype(BF).reshape(4, 8, 16, 256)
            padded[:, 1:9, 48:64, :] = mm(spread, rhs[0:32]).astype(BF).reshape(4, 8, 16, 256)
        if 0 in rows:
            for side, lanes in ((lhs, slice(0, 16)), (rhs, slice(48, 64))):
                ends = mm(corner, side[32:64]).astype(BF).reshape(2, 4, 16, 256)
                padded[:, 0, lanes, :] = ends[0]
                padded[:, 9, lanes, :] = ends[1]
        for t in range(4):
            for r in rows:
                for c in range(3):
                    if c != 1 or centre:
                        out[c, t, r * 32:r * 32 + 32, :] = padded[t, r, 15 + c:47 + c, :]

    middle, ends = tuple(range(1, 9)), (0, 9)

    zero_rows = jnp.zeros((32, 256), BF)
    for c in range(3):
        for t in range(4):
            for r in ends:
                xc[c, t, r * 32:r * 32 + 32, :] = zero_rows
    loads[0].wait()
    cols[...] = mm(select, tile[:, 1:9, 16:48, :].reshape(1024, 256)).astype(BF)
    pl.semaphore_wait(barrier, count)
    halo = halo_copies(tile, cols, left, right, hs, hr)
    for i in (2, 3, 0, 1, 4, 5, 6, 7):
        pl.when(halo[i][0])(halo[i][1].start)
    for t in range(4):
        for r in middle:
            xc[1, t, r * 32:r * 32 + 32, :] = tile[t, r, 16:48, :]

    def x_copy(i):
        ref = (lambda b: (b.at[1, :, 32:288], b.at[0, :, 32:288], b.at[2, :, 32:288], b.at[:, :, 0:32], b.at[:, :, 288:320])[i])
        return pltpu.make_async_remote_copy(
            src_ref=ref(xc), dst_ref=ref(xc2), send_sem=xcs, recv_sem=xcr, device_id=other, device_id_type=MESH)

    loads[1].wait()

    def forward(t, columns):
        total = None
        for f, a in FOLD[t]:
            for b in range(3):
                for c in columns:
                    lanes = slice(c * 256, c * 256 + 256)
                    weight = w_ref[a * 3 + b, lanes] if a < 3 else wsum[(a - 3) * 3 + b, lanes]
                    term = mm(xc[c, f, b * 32:b * 32 + 256, :], weight)
                    total = term if total is None else total + term
        return total

    for t in (3, 2):
        acc_ref[t] = forward(t, (1,))
    for b in range(3):
        two = w_ref[b].astype(F32) + w_ref[3 + b].astype(F32)
        wsum[b] = two.astype(BF)
        wsum[3 + b] = (two + w_ref[6 + b].astype(F32)).astype(BF)
    for t in (1, 0):
        acc_ref[t] = forward(t, (1,))
    halo_wait(tile, left, right, hr, (2, 3))
    shifted(tile, left, right, xc, middle, False)
    for i in range(3):
        x_copy(i).start()
    for t in range(4):
        acc_ref[t] += forward(t, (0, 2))
    halo_wait(tile, left, right, hr, (0, 1, 4, 5, 6, 7))
    shifted(tile, left, right, xc, ends, True)
    x_copy(3).start()
    x_copy(4).start()
    for side, (lo, b) in enumerate(((0, 0), (288, 2))):
        total = None
        for a in range(3):
            for c in range(3):
                rows = jnp.concatenate([xc[c, max(t + a - 2, 0), lo:lo + 32, :] for t in range(4)], axis=0)
                term = mm(rows, w_ref[a * 3 + b, c * 256:c * 256 + 256])
                total = term if total is None else total + term
        fix_ref[side] = total
    loads[2].wait()

    def g_copy(t):
        return pltpu.make_async_remote_copy(
            src_ref=gt.at[:, 1 - core, :, t * 256:t * 256 + 256], dst_ref=gt2.at[:, :, t * 256:t * 256 + 256],
            send_sem=gts, recv_sem=gtr, device_id=other, device_id_type=MESH)

    for t in range(4):
        acc_ref[t, 0:32] += fix_ref[0, t * 32:t * 32 + 32]
        acc_ref[t, 224:256] += fix_ref[1, t * 32:t * 32 + 32]
        acc = acc_ref[t]
        logistic = jax.nn.sigmoid(acc)
        own = tile[t, 1:9, 16:48, :].reshape(256, 256).astype(F32)
        bo[t] = (own + acc * logistic).astype(BF).reshape(8, 32, 256)
        grad = cot[t].reshape(256, 256).astype(F32) * logistic * (1.0 + acc * (1.0 - logistic))
        grad = grad.astype(BF)
        gtile[t, 1:9, 16:48, :] = grad.reshape(8, 32, 256)
        gt[:, :, :, t * 256:t * 256 + 256] = grad.T.reshape(8, 2, 16, 256)
        g_copy(t).start()

    low = iota((128, 128), 1) < 64

    def tap_term(tap, both):
        a, b, c = tap // 9, (tap // 3) % 3, tap % 3
        total = None
        for mine in both:
            for t in range(4):
                lanes = slice(t * 256, t * 256 + 256)
                one = gt[:, core, :, lanes] if mine else gt2[:, :, lanes]
                window = (xc if mine else xc2)[c, max(t + a - 2, 0), b * 32:b * 32 + 256, :]
                term = mm(one.reshape(128, 256), window)
                total = term if total is None else total + term
        return total

    def store_pair(p, by_y):
        for half in range(2):
            lanes = slice(half * 128, half * 128 + 128)
            one, two = hold[p % 4, 0, :, lanes], hold[p % 4, 1, :, lanes]
            both = (jnp.where(low, one, pltpu.roll(two, 64, 1)), jnp.where(low, pltpu.roll(one, 64, 1), two))
            for k, block in enumerate(both):
                for zz in range(2):
                    for yy in range(4):
                        rows = block[(zz * 4 + yy) * 16:(zz * 4 + yy) * 16 + 16]
                        i, j = (yy, 2 * half + k) if by_y else (2 * half + k, yy)
                        part[p, i, j, zz * 16:zz * 16 + 16] = rows
                        partb[p, i, j, zz * 16:zz * 16 + 16] = rows.astype(BF)

    def arrived(ref, sem):
        pltpu.make_async_copy(ref, ref, sem).wait()

    def first_copy(p, d, by_y):
        return pltpu.make_async_remote_copy(
            src_ref=partb.at[p, ((y if by_y else x) + d) % 4], dst_ref=r1.at[p, d - 1],
            send_sem=s1s, recv_sem=s1r.at[p // 4],
            device_id=device(dy=d) if by_y else device(dx=d), device_id_type=MESH)

    def second_copy(p, d, by_y, q):
        return pltpu.make_async_remote_copy(
            src_ref=s1b.at[p, ((y if by_y else x) + d) % 4], dst_ref=r2.at[p, d - 1],
            send_sem=s2s, recv_sem=s2r.at[q],
            device_id=device(dy=d) if by_y else device(dx=d), device_id_type=MESH)

    def third_copy(q, d):
        nz = (z + d) % 8
        return pltpu.make_async_remote_copy(
            src_ref=ob.at[nz % 4, nz // 4, q], dst_ref=r3.at[q, d - 1], send_sem=s3s, recv_sem=s3r.at[q],
            device_id=device(dz=d), device_id_type=MESH)

    def over_pairs(q, body):
        @pl.loop(2 * q, min(2 * q + 2, PAIRS // 2))
        def _(i):
            for k in range(2):
                body(2 * i + k, k == 0)

    def own_terms(pairs):
        for p in pairs:
            for i in range(2):
                hold[p, i] = tap_term(2 * p + i, (True,))

    def pair_terms(p):
        for i in range(2):
            tap = min(2 * p + i, 26)
            hold[p % 4, i] = hold[p, i] + tap_term(tap, (False,)) if p < 4 else tap_term(tap, (True, False))

    def weight_group(done, new):
        for p in new:
            pair_terms(p)
        for p in done:
            store_pair(p, p % 2 == 0)
        for p in done:
            for d in (1, 3, 2):
                first_copy(p, d, p % 2 == 0).start()

    def first_sum(q):
        def body(p, by_y):
            total = part[p, y if by_y else x]
            for d in range(3):
                total = total + r1[p, d].astype(F32)
            s1[p] = total
            s1b[p] = total.astype(BF)
            for d in (1, 3, 2):
                second_copy(p, d, not by_y, q).start()
        arrived(r1.at[4 * q:min(4 * q + 4, PAIRS)], s1r.at[q])
        over_pairs(q, body)

    lane = iota((32, 128), 1)

    def exchange(one, two, width):
        lower = (lane // width) % 2 == 0
        return (jnp.where(lower, one, pltpu.roll(two, width, 1)),
                jnp.where(lower, pltpu.roll(one, 128 - width, 1), two))

    def second_sum(q):
        def body(p, by_y):
            total = s1[p, x if by_y else y]
            for d in range(3):
                total = total + r2[p, d].astype(F32)
            s2[p] = total
        arrived(r2.at[4 * q:min(4 * q + 4, PAIRS)], s2r.at[q])
        over_pairs(q, body)
        v = [s2[4 * q + i] if 4 * q + i < PAIRS else jnp.zeros((32, 128), F32) for i in range(4)]
        v[0], v[1] = exchange(v[0], v[1], 16)
        v[2], v[3] = exchange(v[2], v[3], 16)
        v[0], v[2] = exchange(v[0], v[2], 32)
        v[1], v[3] = exchange(v[1], v[3], 32)
        for i in range(4):
            for zz in range(2):
                of[i, zz, q] = v[i][zz * 16:zz * 16 + 16]
                ob[i, zz, q] = v[i][zz * 16:zz * 16 + 16].astype(BF)
        for d in (4, 3, 5, 2, 6, 1, 7):
            third_copy(q, d).start()

    def feature_gradient(t):
        terms = [(t + 2 - a, a) for a in range(3) if t + 2 - a < 4] if t else [(2, 0), (1, 3), (0, 4)]
        total = None
        for f, a in terms:
            for b in range(3):
                for c in range(3):
                    index = a * 3 + 2 - b if a < 3 else (a - 3) * 3 + 2 - b
                    weight = (w_ref if a < 3 else wsum)[index, (2 - c) * 256:(2 - c) * 256 + 256, :]
                    term = nt(xg[c, f, b * 32:b * 32 + 256, :], weight)
                    total = term if total is None else total + term
        total = total + cot[t].reshape(256, 256).astype(F32)
        fg[t] = total.astype(BF).reshape(8, 32, 256)

    for present, copy in halo:
        pl.when(present)(copy.wait_send)
    ghalo = halo_copies(gtile, gcols, gleft, gright, hs, ghr)
    for i in (0, 1):
        pl.when(ghalo[i][0])(ghalo[i][1].start)
    own_terms(range(4))
    arrived(gt2, gtr)
    arrived(xc2, xcr)
    weight_group((), (0,))
    weight_group((0,), (1,))
    weight_group((1,), (2, 3))
    gcols[...] = mm(select, gtile[:, 1:9, 16:48, :].reshape(1024, 256)).astype(BF)
    for i in range(2, 8):
        pl.when(ghalo[i][0])(ghalo[i][1].start)
    weight_group((2, 3), (4, 5))
    weight_group((4, 5), (6, 7))
    weight_group((6, 7), (8, 9))
    weight_group((8, 9), (10, 11))
    bo_out = pltpu.make_async_copy(bo, bo_hbm, local_sem.at[0])
    bo_out.start()
    weight_group((10, 11), (12, 13))
    weight_group((12, 13), ())
    halo_wait(gtile, gleft, gright, ghr, range(8))
    shifted(gtile, gleft, gright, xg, tuple(range(10)), True)
    feature_gradient(3)
    feature_gradient(2)
    for q in range(4):
        first_sum(q)
    second_sum(0)
    second_sum(1)
    feature_gradient(1)
    second_sum(2)
    second_sum(3)
    feature_gradient(0)
    fg_out = pltpu.make_async_copy(fg, fg_hbm, local_sem.at[1])
    fg_out.start()
    for q in range(4):
        arrived(r3.at[q], s3r.at[q])
        total = of[zlo, zhi, q]
        for d in range(7):
            total = total + r3[q, d].astype(F32)
        wg_ref[q] = total * (1.0 / 512.0)

    for present, copy in ghalo:
        pl.when(present)(copy.wait_send)
    arrived(xc, xcs)
    arrived(gt2, gts)
    arrived(r1, s1s)
    arrived(r2, s2s)
    arrived(r3, s3s)
    bo_out.wait()
    fg_out.wait()


def finish(bo_in, fg_in, packed, bo_out, fg_out, wg_out, flat, sems):
    copies = [pltpu.make_async_copy(bo_in, bo_out, sems.at[0]), pltpu.make_async_copy(fg_in, fg_out, sems.at[1])]
    for copy in copies:
        copy.start()
    for q in range(4):
        flipped = packed[q].T
        for e in range(8):
            tap = 8 * q + 2 * (e % 4) + e // 4
            flat[tap * 16:tap * 16 + 16, :] = flipped[e * 16:e * 16 + 16, :]
    for k in range(16):
        wg_out[k] = flat[pl.ds(k, 32, stride=16), :].T[:, :27]
    for copy in copies:
        copy.wait()


def per_device(features, weights, cotangent):
    dma = pltpu.SemaphoreType.DMA
    anywhere = pl.BlockSpec(memory_space=pl.ANY)
    vmem = pl.BlockSpec(memory_space=pltpu.VMEM)
    block = jax.ShapeDtypeStruct((4, 8, 32, 256), BF)
    block_out, feature_grad, packed = pl.pallas_call(
        kernel,
        out_shape=(block, block, jax.ShapeDtypeStruct((4, 16, 128), F32)),
        in_specs=[anywhere] * 3,
        out_specs=(anywhere, anywhere, vmem),
        scratch_shapes=[
            pltpu.VMEM((9, 768, 256), BF), pltpu.VMEM((6, 768, 256), BF),
            pltpu.VMEM((4, 10, 64, 256), BF), pltpu.VMEM((4, 10, 64, 256), BF),
            pltpu.VMEM((3, 4, 320, 256), BF), pltpu.VMEM((3, 4, 320, 256), BF), pltpu.VMEM((3, 4, 320, 256), BF),
            pltpu.VMEM((4, 8, 32, 256), BF), pltpu.VMEM((4, 8, 32, 256), BF), pltpu.VMEM((4, 8, 32, 256), BF),
            pltpu.VMEM((4, 256, 256), F32), pltpu.VMEM((2, 128, 256), F32), pltpu.VMEM((4, 2, 128, 256), F32),
            pltpu.VMEM((8, 2, 16, 1024), BF), pltpu.VMEM((8, 16, 1024), BF),
            pltpu.VMEM((128, 256), BF), pltpu.VMEM((128, 256), BF),
            pltpu.VMEM((64, 256), BF), pltpu.VMEM((64, 256), BF), pltpu.VMEM((64, 256), BF), pltpu.VMEM((64, 256), BF),
            pltpu.VMEM((PAIRS, 4, 4, 32, 128), F32), pltpu.VMEM((PAIRS, 4, 4, 32, 128), BF),
            pltpu.VMEM((PAIRS, 3, 4, 32, 128), BF),
            pltpu.VMEM((PAIRS, 4, 32, 128), F32), pltpu.VMEM((PAIRS, 4, 32, 128), BF),
            pltpu.VMEM((PAIRS, 3, 32, 128), BF), pltpu.VMEM((PAIRS, 32, 128), F32),
            pltpu.VMEM((4, 2, 4, 16, 128), F32), pltpu.VMEM((4, 2, 4, 16, 128), BF), pltpu.VMEM((4, 7, 16, 128), BF),
            dma((3,)), dma((8,)), dma((8,)), dma((8,)), dma, dma, dma, dma,
            dma, dma((4,)), dma, dma((4,)), dma, dma((4,)),
        ],
        compiler_params=pltpu.CompilerParams(collective_id=0, has_side_effects=True, vmem_limit_bytes=60 << 20),
        cost_estimate=pl.CostEstimate(flops=9_000_000_000, bytes_accessed=6_000_000, transcendentals=300_000),
        name="conv_block",
    )(features, weights.reshape(9, 768, 256), cotangent)
    block_out, feature_grad, grads = pl.pallas_call(
        finish,
        out_shape=(block, block, jax.ShapeDtypeStruct((16, 16, 27), F32)),
        in_specs=[vmem] * 3,
        out_specs=(anywhere, anywhere, vmem),
        scratch_shapes=[pltpu.VMEM((512, 16), F32), dma((2,))],
        name="finish",
    )(block_out, feature_grad, packed)
    return block_out, feature_grad, grads.transpose(2, 0, 1)


def solution(mesh):
    in_specs = (P(None, "ha", "wa", None), P(), P(None, "ha", "wa", None))
    out_specs = (P(None, "ha", "wa", None), P(None, "ha", "wa", None), P(None, "ha", "wa"))
    return jax.shard_map(
        per_device, mesh=mesh, in_specs=in_specs, out_specs=out_specs, check_vma=False
    )
```

```python
import jax
import jax.numpy as jnp
from jax import lax
from jax.experimental import pallas as pl
from jax.experimental.pallas import tpu as pltpu
from jax.sharding import PartitionSpec as P

MESH = pl.DeviceIdType.MESH
BF, F32 = jnp.bfloat16, jnp.float32
PAIRS = 14
FOLD = (((0, 4),), ((0, 3), (1, 2)), ((0, 0), (1, 1), (2, 2)), ((1, 0), (2, 1), (3, 2)))


def mm(a, b):
    return jnp.dot(a, b, preferred_element_type=F32)


def nt(a, b):
    return lax.dot_general(a, b, (((1,), (1,)), ((), ())), preferred_element_type=F32)


def iota(shape, dim):
    return lax.broadcasted_iota(jnp.int32, shape, dim)


def kernel(
    feat_hbm, w_hbm, cot_hbm,
    bo_hbm, fg_hbm, wg_ref,
    w_ref, wsum, tile, gtile, xc, xc2, xg, cot, bo, fg, acc_ref, fix_ref, hold, gt, gt2,
    cols, gcols, left, right, gleft, gright,
    part, partb, r1, s1, s1b, r2, s2, of, ob, r3,
    local_sem, hs, hr, ghr, xcs, xcr, gts, gtr, s1s, s1r, s2s, s2r, s3s, s3r,
):
    ha, wa = lax.axis_index("ha"), lax.axis_index("wa")
    x, zlo = ha // 4, ha % 4
    zhi, y, core = wa // 8, (wa // 2) % 4, wa % 2
    z = zhi * 4 + zlo

    def device(dx=0, dy=0, dz=0, dc=0):
        nx, ny, nz, nc = (x + dx) % 4, (y + dy) % 4, (z + dz) % 8, (core + dc) % 2
        return (nx * 4 + nz % 4, (nz // 4) * 8 + ny * 2 + nc)

    other = device(dc=1)
    north, south, west, east = ha > 0, ha < 15, wa > 0, wa < 15
    sides = (
        (north, -1, 0), (south, 1, 0), (west, 0, -1), (east, 0, 1),
        (north & west, -1, -1), (north & east, -1, 1), (south & west, 1, -1), (south & east, 1, 1),
    )

    loads = [
        pltpu.make_async_copy(feat_hbm, tile.at[:, 1:9, 16:48, :], local_sem.at[0]),
        pltpu.make_async_copy(w_hbm, w_ref, local_sem.at[1]),
        pltpu.make_async_copy(cot_hbm, cot, local_sem.at[2]),
    ]
    for copy in loads:
        copy.start()

    barrier = pltpu.get_barrier_semaphore()
    peers = [device(dz=d) for d in (4, 3, 5, 2, 6)] + [device(dy=2), device(dx=2)]
    peers += [device(dz=d) for d in (1, 7)] + [device(dy=d) for d in (1, 3)] + [device(dx=d) for d in (1, 3)] + [other]
    for peer in peers[:5]:
        pl.semaphore_signal(barrier, inc=1, device_id=peer, device_id_type=MESH)
    count = 14
    for present, dr, dc in sides:
        @pl.when(present)
        def _():
            pl.semaphore_signal(barrier, inc=1, device_id=(ha + dr, wa + dc), device_id_type=MESH)
        count = count + present.astype(jnp.int32)
    for peer in peers[5:]:
        pl.semaphore_signal(barrier, inc=1, device_id=peer, device_id_type=MESH)

    m, n = iota((128, 1024), 0), iota((128, 1024), 1)
    column = jnp.where(m < 64, 31, 0)
    place = m % 64
    pick = jnp.where(place < 32, place * 32, jnp.where(place < 48, (place - 32) * 256, (place - 48) * 256 + 224)) + column
    select = jnp.where(pick == n, 1.0, 0.0).astype(BF)
    m, n = iota((512, 32), 0), iota((512, 32), 1)
    spread = jnp.where(m // 16 == n, 1.0, 0.0).astype(BF)
    m, n = iota((128, 32), 0), iota((128, 32), 1)
    corner = jnp.where(m // 64 * 16 + (m % 64) // 16 == n, 1.0, 0.0).astype(BF)

    def halo_copies(padded, packed, lhs, rhs, send, recv):
        row_src = {-1: padded.at[:, 1, 16:48, :], 1: padded.at[:, 8, 16:48, :]}
        row_dst = {-1: padded.at[:, 9, 16:48, :], 1: padded.at[:, 0, 16:48, :]}
        copies = []
        for i, (present, dr, dc) in enumerate(sides):
            if dc == 0:
                src, dst = row_src[dr], row_dst[dr]
            else:
                base = 0 if dc == 1 else 64
                target = lhs if dc == 1 else rhs
                if dr == 0:
                    src, dst = packed.at[base:base + 32], target.at[0:32]
                elif dr == -1:
                    src, dst = packed.at[base + 32:base + 48], target.at[48:64]
                else:
                    src, dst = packed.at[base + 48:base + 64], target.at[32:48]
            back = {(-1, 0): 1, (1, 0): 0, (0, -1): 3, (0, 1): 2, (-1, -1): 7, (-1, 1): 6, (1, -1): 5, (1, 1): 4}[(dr, dc)]
            copies.append((present, pltpu.make_async_remote_copy(
                src_ref=src, dst_ref=dst, send_sem=send.at[i], recv_sem=recv.at[back],
                device_id=(ha + dr, wa + dc), device_id_type=MESH)))
        return copies

    def halo_wait(padded, lhs, rhs, recv, which):
        landing = (
            padded.at[:, 0, 16:48, :], padded.at[:, 9, 16:48, :], lhs.at[0:32], rhs.at[0:32],
            lhs.at[32:48], rhs.at[32:48], lhs.at[48:64], rhs.at[48:64],
        )
        for i in which:
            present, ref = sides[i][0], landing[i]

            @pl.when(present)
            def _():
                pltpu.make_async_copy(ref, ref, recv.at[i]).wait()

            @pl.when(jnp.logical_not(present))
            def _():
                ref[...] = jnp.zeros(ref.shape, BF)

    def shifted(padded, lhs, rhs, out, rows, centre):
        if 1 in rows:
            padded[:, 1:9, 0:16, :] = mm(spread, lhs[0:32]).astype(BF).reshape(4, 8, 16, 256)
            padded[:, 1:9, 48:64, :] = mm(spread, rhs[0:32]).astype(BF).reshape(4, 8, 16, 256)
        if 0 in rows:
            for side, lanes in ((lhs, slice(0, 16)), (rhs, slice(48, 64))):
                ends = mm(corner, side[32:64]).astype(BF).reshape(2, 4, 16, 256)
                padded[:, 0, lanes, :] = ends[0]
                padded[:, 9, lanes, :] = ends[1]
        for t in range(4):
            for r in rows:
                for c in range(3):
                    if c != 1 or centre:
                        out[c, t, r * 32:r * 32 + 32, :] = padded[t, r, 15 + c:47 + c, :]

    middle, ends = tuple(range(1, 9)), (0, 9)

    zero_rows = jnp.zeros((32, 256), BF)
    for c in range(3):
        for t in range(4):
            for r in ends:
                xc[c, t, r * 32:r * 32 + 32, :] = zero_rows
    loads[0].wait()
    cols[...] = mm(select, tile[:, 1:9, 16:48, :].reshape(1024, 256)).astype(BF)
    pl.semaphore_wait(barrier, count)
    halo = halo_copies(tile, cols, left, right, hs, hr)
    for i in (2, 3, 0, 1, 4, 5, 6, 7):
        pl.when(halo[i][0])(halo[i][1].start)
    for t in range(4):
        for r in middle:
            xc[1, t, r * 32:r * 32 + 32, :] = tile[t, r, 16:48, :]

    def x_copy(i):
        ref = (lambda b: (b.at[1, :, 32:288], b.at[0, :, 32:288], b.at[2, :, 32:288], b.at[:, :, 0:32], b.at[:, :, 288:320])[i])
        return pltpu.make_async_remote_copy(
            src_ref=ref(xc), dst_ref=ref(xc2), send_sem=xcs, recv_sem=xcr, device_id=other, device_id_type=MESH)

    loads[1].wait()

    def forward(t, columns):
        total = None
        for f, a in FOLD[t]:
            for b in range(3):
                for c in columns:
                    lanes = slice(c * 256, c * 256 + 256)
                    weight = w_ref[a * 3 + b, lanes] if a < 3 else wsum[(a - 3) * 3 + b, lanes]
                    term = mm(xc[c, f, b * 32:b * 32 + 256, :], weight)
                    total = term if total is None else total + term
        return total

    for t in (3, 2):
        acc_ref[t] = forward(t, (1,))
    for b in range(3):
        two = w_ref[b].astype(F32) + w_ref[3 + b].astype(F32)
        wsum[b] = two.astype(BF)
        wsum[3 + b] = (two + w_ref[6 + b].astype(F32)).astype(BF)
    for t in (1, 0):
        acc_ref[t] = forward(t, (1,))
    halo_wait(tile, left, right, hr, (2, 3))
    shifted(tile, left, right, xc, middle, False)
    for i in range(3):
        x_copy(i).start()
    for t in range(4):
        acc_ref[t] += forward(t, (0, 2))
    halo_wait(tile, left, right, hr, (0, 1, 4, 5, 6, 7))
    shifted(tile, left, right, xc, ends, True)
    x_copy(3).start()
    x_copy(4).start()
    for side, (lo, b) in enumerate(((0, 0), (288, 2))):
        total = None
        for a in range(3):
            for c in range(3):
                rows = jnp.concatenate([xc[c, max(t + a - 2, 0), lo:lo + 32, :] for t in range(4)], axis=0)
                term = mm(rows, w_ref[a * 3 + b, c * 256:c * 256 + 256])
                total = term if total is None else total + term
        fix_ref[side] = total
    loads[2].wait()

    def g_copy(t):
        return pltpu.make_async_remote_copy(
            src_ref=gt.at[:, 1 - core, :, t * 256:t * 256 + 256], dst_ref=gt2.at[:, :, t * 256:t * 256 + 256],
            send_sem=gts, recv_sem=gtr, device_id=other, device_id_type=MESH)

    for t in range(4):
        acc_ref[t, 0:32] += fix_ref[0, t * 32:t * 32 + 32]
        acc_ref[t, 224:256] += fix_ref[1, t * 32:t * 32 + 32]
        acc = acc_ref[t]
        logistic = jax.nn.sigmoid(acc)
        own = tile[t, 1:9, 16:48, :].reshape(256, 256).astype(F32)
        bo[t] = (own + acc * logistic).astype(BF).reshape(8, 32, 256)
        grad = cot[t].reshape(256, 256).astype(F32) * logistic * (1.0 + acc * (1.0 - logistic))
        grad = grad.astype(BF)
        gtile[t, 1:9, 16:48, :] = grad.reshape(8, 32, 256)
        gt[:, :, :, t * 256:t * 256 + 256] = grad.T.reshape(8, 2, 16, 256)
        g_copy(t).start()

    low = iota((128, 128), 1) < 64

    def tap_term(tap, both):
        a, b, c = tap // 9, (tap // 3) % 3, tap % 3
        total = None
        for mine in both:
            for t in range(4):
                lanes = slice(t * 256, t * 256 + 256)
                one = gt[:, core, :, lanes] if mine else gt2[:, :, lanes]
                window = (xc if mine else xc2)[c, max(t + a - 2, 0), b * 32:b * 32 + 256, :]
                term = mm(one.reshape(128, 256), window)
                total = term if total is None else total + term
        return total

    def store_pair(p, by_y):
        for half in range(2):
            lanes = slice(half * 128, half * 128 + 128)
            one, two = hold[p % 4, 0, :, lanes], hold[p % 4, 1, :, lanes]
            both = (jnp.where(low, one, pltpu.roll(two, 64, 1)), jnp.where(low, pltpu.roll(one, 64, 1), two))
            for k, block in enumerate(both):
                for zz in range(2):
                    for yy in range(4):
                        rows = block[(zz * 4 + yy) * 16:(zz * 4 + yy) * 16 + 16]
                        i, j = (yy, 2 * half + k) if by_y else (2 * half + k, yy)
                        part[p, i, j, zz * 16:zz * 16 + 16] = rows
                        partb[p, i, j, zz * 16:zz * 16 + 16] = rows.astype(BF)

    def arrived(ref, sem):
        pltpu.make_async_copy(ref, ref, sem).wait()

    def first_copy(p, d, by_y):
        return pltpu.make_async_remote_copy(
            src_ref=partb.at[p, ((y if by_y else x) + d) % 4], dst_ref=r1.at[p, d - 1],
            send_sem=s1s, recv_sem=s1r.at[p // 4],
            device_id=device(dy=d) if by_y else device(dx=d), device_id_type=MESH)

    def second_copy(p, d, by_y, q):
        return pltpu.make_async_remote_copy(
            src_ref=s1b.at[p, ((y if by_y else x) + d) % 4], dst_ref=r2.at[p, d - 1],
            send_sem=s2s, recv_sem=s2r.at[q],
            device_id=device(dy=d) if by_y else device(dx=d), device_id_type=MESH)

    def third_copy(q, d):
        nz = (z + d) % 8
        return pltpu.make_async_remote_copy(
            src_ref=ob.at[nz % 4, nz // 4, q], dst_ref=r3.at[q, d - 1], send_sem=s3s, recv_sem=s3r.at[q],
            device_id=device(dz=d), device_id_type=MESH)

    def over_pairs(q, body):
        @pl.loop(2 * q, min(2 * q + 2, PAIRS // 2))
        def _(i):
            for k in range(2):
                body(2 * i + k, k == 0)

    def own_terms(pairs):
        for p in pairs:
            for i in range(2):
                hold[p, i] = tap_term(2 * p + i, (True,))

    def pair_terms(p):
        for i in range(2):
            tap = min(2 * p + i, 26)
            hold[p % 4, i] = hold[p, i] + tap_term(tap, (False,)) if p < 4 else tap_term(tap, (True, False))

    def weight_group(done, new):
        for p in new:
            pair_terms(p)
        for p in done:
            store_pair(p, p % 2 == 0)
        for p in done:
            for d in (1, 3, 2):
                first_copy(p, d, p % 2 == 0).start()

    def first_sum(q):
        def body(p, by_y):
            total = part[p, y if by_y else x]
            for d in range(3):
                total = total + r1[p, d].astype(F32)
            s1[p] = total
            s1b[p] = total.astype(BF)
            for d in (1, 3, 2):
                second_copy(p, d, not by_y, q).start()
        arrived(r1.at[4 * q:min(4 * q + 4, PAIRS)], s1r.at[q])
        over_pairs(q, body)

    lane = iota((32, 128), 1)

    def exchange(one, two, width):
        lower = (lane // width) % 2 == 0
        return (jnp.where(lower, one, pltpu.roll(two, width, 1)),
                jnp.where(lower, pltpu.roll(one, 128 - width, 1), two))

    def second_sum(q):
        def body(p, by_y):
            total = s1[p, x if by_y else y]
            for d in range(3):
                total = total + r2[p, d].astype(F32)
            s2[p] = total
        arrived(r2.at[4 * q:min(4 * q + 4, PAIRS)], s2r.at[q])
        over_pairs(q, body)
        v = [s2[4 * q + i] if 4 * q + i < PAIRS else jnp.zeros((32, 128), F32) for i in range(4)]
        v[0], v[1] = exchange(v[0], v[1], 16)
        v[2], v[3] = exchange(v[2], v[3], 16)
        v[0], v[2] = exchange(v[0], v[2], 32)
        v[1], v[3] = exchange(v[1], v[3], 32)
        for i in range(4):
            for zz in range(2):
                of[i, zz, q] = v[i][zz * 16:zz * 16 + 16]
                ob[i, zz, q] = v[i][zz * 16:zz * 16 + 16].astype(BF)
        for d in (4, 3, 5, 2, 6, 1, 7):
            third_copy(q, d).start()

    def feature_gradient(t):
        terms = [(t + 2 - a, a) for a in range(3) if t + 2 - a < 4] if t else [(2, 0), (1, 3), (0, 4)]
        total = None
        for f, a in terms:
            for b in range(3):
                for c in range(3):
                    index = a * 3 + 2 - b if a < 3 else (a - 3) * 3 + 2 - b
                    weight = (w_ref if a < 3 else wsum)[index, (2 - c) * 256:(2 - c) * 256 + 256, :]
                    term = nt(xg[c, f, b * 32:b * 32 + 256, :], weight)
                    total = term if total is None else total + term
        total = total + cot[t].reshape(256, 256).astype(F32)
        fg[t] = total.astype(BF).reshape(8, 32, 256)

    for present, copy in halo:
        pl.when(present)(copy.wait_send)
    ghalo = halo_copies(gtile, gcols, gleft, gright, hs, ghr)
    for i in (0, 1):
        pl.when(ghalo[i][0])(ghalo[i][1].start)
    own_terms(range(4))
    arrived(gt2, gtr)
    arrived(xc2, xcr)
    weight_group((), (0,))
    weight_group((0,), (1,))
    weight_group((1,), (2, 3))
    gcols[...] = mm(select, gtile[:, 1:9, 16:48, :].reshape(1024, 256)).astype(BF)
    for i in range(2, 8):
        pl.when(ghalo[i][0])(ghalo[i][1].start)
    weight_group((2, 3), (4, 5))
    weight_group((4, 5), (6, 7))
    weight_group((6, 7), (8, 9))
    weight_group((8, 9), (10, 11))
    bo_out = pltpu.make_async_copy(bo, bo_hbm, local_sem.at[0])
    bo_out.start()
    weight_group((10, 11), (12, 13))
    weight_group((12, 13), ())
    first_sum(0)
    halo_wait(gtile, gleft, gright, ghr, range(8))
    shifted(gtile, gleft, gright, xg, tuple(range(10)), True)
    feature_gradient(3)
    first_sum(1)
    feature_gradient(2)
    first_sum(2)
    first_sum(3)
    second_sum(0)
    second_sum(1)
    feature_gradient(1)
    second_sum(2)
    second_sum(3)
    feature_gradient(0)
    fg_out = pltpu.make_async_copy(fg, fg_hbm, local_sem.at[1])
    fg_out.start()
    for q in range(4):
        arrived(r3.at[q], s3r.at[q])
        total = of[zlo, zhi, q]
        for d in range(7):
            total = total + r3[q, d].astype(F32)
        wg_ref[q] = total * (1.0 / 512.0)

    for present, copy in ghalo:
        pl.when(present)(copy.wait_send)
    arrived(xc, xcs)
    arrived(gt2, gts)
    arrived(r1, s1s)
    arrived(r2, s2s)
    arrived(r3, s3s)
    bo_out.wait()
    fg_out.wait()


def finish(bo_in, fg_in, packed, bo_out, fg_out, wg_out, flat, sems):
    copies = [pltpu.make_async_copy(bo_in, bo_out, sems.at[0]), pltpu.make_async_copy(fg_in, fg_out, sems.at[1])]
    for copy in copies:
        copy.start()
    for q in range(4):
        flipped = packed[q].T
        for e in range(8):
            tap = 8 * q + 2 * (e % 4) + e // 4
            flat[tap * 16:tap * 16 + 16, :] = flipped[e * 16:e * 16 + 16, :]
    for k in range(16):
        wg_out[k] = flat[pl.ds(k, 32, stride=16), :].T[:, :27]
    for copy in copies:
        copy.wait()


def per_device(features, weights, cotangent):
    dma = pltpu.SemaphoreType.DMA
    anywhere = pl.BlockSpec(memory_space=pl.ANY)
    vmem = pl.BlockSpec(memory_space=pltpu.VMEM)
    block = jax.ShapeDtypeStruct((4, 8, 32, 256), BF)
    block_out, feature_grad, packed = pl.pallas_call(
        kernel,
        out_shape=(block, block, jax.ShapeDtypeStruct((4, 16, 128), F32)),
        in_specs=[anywhere] * 3,
        out_specs=(anywhere, anywhere, vmem),
        scratch_shapes=[
            pltpu.VMEM((9, 768, 256), BF), pltpu.VMEM((6, 768, 256), BF),
            pltpu.VMEM((4, 10, 64, 256), BF), pltpu.VMEM((4, 10, 64, 256), BF),
            pltpu.VMEM((3, 4, 320, 256), BF), pltpu.VMEM((3, 4, 320, 256), BF), pltpu.VMEM((3, 4, 320, 256), BF),
            pltpu.VMEM((4, 8, 32, 256), BF), pltpu.VMEM((4, 8, 32, 256), BF), pltpu.VMEM((4, 8, 32, 256), BF),
            pltpu.VMEM((4, 256, 256), F32), pltpu.VMEM((2, 128, 256), F32), pltpu.VMEM((4, 2, 128, 256), F32),
            pltpu.VMEM((8, 2, 16, 1024), BF), pltpu.VMEM((8, 16, 1024), BF),
            pltpu.VMEM((128, 256), BF), pltpu.VMEM((128, 256), BF),
            pltpu.VMEM((64, 256), BF), pltpu.VMEM((64, 256), BF), pltpu.VMEM((64, 256), BF), pltpu.VMEM((64, 256), BF),
            pltpu.VMEM((PAIRS, 4, 4, 32, 128), F32), pltpu.VMEM((PAIRS, 4, 4, 32, 128), BF),
            pltpu.VMEM((PAIRS, 3, 4, 32, 128), BF),
            pltpu.VMEM((PAIRS, 4, 32, 128), F32), pltpu.VMEM((PAIRS, 4, 32, 128), BF),
            pltpu.VMEM((PAIRS, 3, 32, 128), BF), pltpu.VMEM((PAIRS, 32, 128), F32),
            pltpu.VMEM((4, 2, 4, 16, 128), F32), pltpu.VMEM((4, 2, 4, 16, 128), BF), pltpu.VMEM((4, 7, 16, 128), BF),
            dma((3,)), dma((8,)), dma((8,)), dma((8,)), dma, dma, dma, dma,
            dma, dma((4,)), dma, dma((4,)), dma, dma((4,)),
        ],
        compiler_params=pltpu.CompilerParams(collective_id=0, has_side_effects=True, vmem_limit_bytes=60 << 20),
        cost_estimate=pl.CostEstimate(flops=9_000_000_000, bytes_accessed=6_000_000, transcendentals=300_000),
        name="conv_block",
    )(features, weights.reshape(9, 768, 256), cotangent)
    block_out, feature_grad, grads = pl.pallas_call(
        finish,
        out_shape=(block, block, jax.ShapeDtypeStruct((16, 16, 27), F32)),
        in_specs=[vmem] * 3,
        out_specs=(anywhere, anywhere, vmem),
        scratch_shapes=[pltpu.VMEM((512, 16), F32), dma((2,))],
        name="finish",
    )(block_out, feature_grad, packed)
    return block_out, feature_grad, grads.transpose(2, 0, 1)


def solution(mesh):
    in_specs = (P(None, "ha", "wa", None), P(), P(None, "ha", "wa", None))
    out_specs = (P(None, "ha", "wa", None), P(None, "ha", "wa", None), P(None, "ha", "wa"))
    return jax.shard_map(
        per_device, mesh=mesh, in_specs=in_specs, out_specs=out_specs, check_vma=False
    )
```

```python
import jax
import jax.numpy as jnp
from jax import lax
from jax.experimental import pallas as pl
from jax.experimental.pallas import tpu as pltpu
from jax.sharding import PartitionSpec as P

MESH = pl.DeviceIdType.MESH
BF, F32 = jnp.bfloat16, jnp.float32
PAIRS = 14
FOLD = (((0, 4),), ((0, 3), (1, 2)), ((0, 0), (1, 1), (2, 2)), ((1, 0), (2, 1), (3, 2)))


def mm(a, b):
    return jnp.dot(a, b, preferred_element_type=F32)


def nt(a, b):
    return lax.dot_general(a, b, (((1,), (1,)), ((), ())), preferred_element_type=F32)


def iota(shape, dim):
    return lax.broadcasted_iota(jnp.int32, shape, dim)


def kernel(
    feat_hbm, w_hbm, cot_hbm,
    bo_hbm, fg_hbm, wg_ref,
    w_ref, wsum, tile, gtile, xc, xc2, xg, cot, bo, fg, acc_ref, fix_ref, hold, gt, gt2,
    cols, gcols, left, right, gleft, gright,
    part, partb, r1, s1, s1b, r2, s2, of, ob, r3,
    local_sem, hs, hr, ghr, xcs, xcr, gts, gtr, s1s, s1r, s2s, s2r, s3s, s3r,
):
    ha, wa = lax.axis_index("ha"), lax.axis_index("wa")
    x, zlo = ha // 4, ha % 4
    zhi, y, core = wa // 8, (wa // 2) % 4, wa % 2
    z = zhi * 4 + zlo

    def device(dx=0, dy=0, dz=0, dc=0):
        nx, ny, nz, nc = (x + dx) % 4, (y + dy) % 4, (z + dz) % 8, (core + dc) % 2
        return (nx * 4 + nz % 4, (nz // 4) * 8 + ny * 2 + nc)

    other = device(dc=1)
    north, south, west, east = ha > 0, ha < 15, wa > 0, wa < 15
    sides = (
        (north, -1, 0), (south, 1, 0), (west, 0, -1), (east, 0, 1),
        (north & west, -1, -1), (north & east, -1, 1), (south & west, 1, -1), (south & east, 1, 1),
    )

    loads = [
        pltpu.make_async_copy(feat_hbm, tile.at[:, 1:9, 16:48, :], local_sem.at[0]),
        pltpu.make_async_copy(w_hbm, w_ref, local_sem.at[1]),
        pltpu.make_async_copy(cot_hbm, cot, local_sem.at[2]),
    ]
    for copy in loads:
        copy.start()

    barrier = pltpu.get_barrier_semaphore()
    count = 14
    for present, dr, dc in sides:
        @pl.when(present)
        def _():
            pl.semaphore_signal(barrier, inc=1, device_id=(ha + dr, wa + dc), device_id_type=MESH)
        count = count + present.astype(jnp.int32)
    peers = [device(dy=d) for d in (1, 2, 3)] + [device(dx=d) for d in (1, 2, 3)]
    peers += [device(dz=d) for d in range(1, 8)] + [other]
    for peer in peers:
        pl.semaphore_signal(barrier, inc=1, device_id=peer, device_id_type=MESH)

    m, n = iota((128, 1024), 0), iota((128, 1024), 1)
    column = jnp.where(m < 64, 31, 0)
    place = m % 64
    pick = jnp.where(place < 32, place * 32, jnp.where(place < 48, (place - 32) * 256, (place - 48) * 256 + 224)) + column
    select = jnp.where(pick == n, 1.0, 0.0).astype(BF)
    m, n = iota((512, 32), 0), iota((512, 32), 1)
    spread = jnp.where(m // 16 == n, 1.0, 0.0).astype(BF)
    m, n = iota((128, 32), 0), iota((128, 32), 1)
    corner = jnp.where(m // 64 * 16 + (m % 64) // 16 == n, 1.0, 0.0).astype(BF)

    def halo_copies(padded, packed, lhs, rhs, send, recv):
        row_src = {-1: padded.at[:, 1, 16:48, :], 1: padded.at[:, 8, 16:48, :]}
        row_dst = {-1: padded.at[:, 9, 16:48, :], 1: padded.at[:, 0, 16:48, :]}
        copies = []
        for i, (present, dr, dc) in enumerate(sides):
            if dc == 0:
                src, dst = row_src[dr], row_dst[dr]
            else:
                base = 0 if dc == 1 else 64
                target = lhs if dc == 1 else rhs
                if dr == 0:
                    src, dst = packed.at[base:base + 32], target.at[0:32]
                elif dr == -1:
                    src, dst = packed.at[base + 32:base + 48], target.at[48:64]
                else:
                    src, dst = packed.at[base + 48:base + 64], target.at[32:48]
            back = {(-1, 0): 1, (1, 0): 0, (0, -1): 3, (0, 1): 2, (-1, -1): 7, (-1, 1): 6, (1, -1): 5, (1, 1): 4}[(dr, dc)]
            copies.append((present, pltpu.make_async_remote_copy(
                src_ref=src, dst_ref=dst, send_sem=send.at[i], recv_sem=recv.at[back],
                device_id=(ha + dr, wa + dc), device_id_type=MESH)))
        return copies

    def halo_wait(padded, lhs, rhs, recv, which):
        landing = (
            padded.at[:, 0, 16:48, :], padded.at[:, 9, 16:48, :], lhs.at[0:32], rhs.at[0:32],
            lhs.at[32:48], rhs.at[32:48], lhs.at[48:64], rhs.at[48:64],
        )
        for i in which:
            present, ref = sides[i][0], landing[i]

            @pl.when(present)
            def _():
                pltpu.make_async_copy(ref, ref, recv.at[i]).wait()

            @pl.when(jnp.logical_not(present))
            def _():
                ref[...] = jnp.zeros(ref.shape, BF)

    def shifted(padded, lhs, rhs, out, rows, centre):
        if 1 in rows:
            padded[:, 1:9, 0:16, :] = mm(spread, lhs[0:32]).astype(BF).reshape(4, 8, 16, 256)
            padded[:, 1:9, 48:64, :] = mm(spread, rhs[0:32]).astype(BF).reshape(4, 8, 16, 256)
        if 0 in rows:
            for side, lanes in ((lhs, slice(0, 16)), (rhs, slice(48, 64))):
                ends = mm(corner, side[32:64]).astype(BF).reshape(2, 4, 16, 256)
                padded[:, 0, lanes, :] = ends[0]
                padded[:, 9, lanes, :] = ends[1]
        for t in range(4):
            for r in rows:
                for c in range(3):
                    if c != 1 or centre:
                        out[c, t, r * 32:r * 32 + 32, :] = padded[t, r, 15 + c:47 + c, :]

    middle, ends = tuple(range(1, 9)), (0, 9)

    zero_rows = jnp.zeros((32, 256), BF)
    for c in range(3):
        for t in range(4):
            for r in ends:
                xc[c, t, r * 32:r * 32 + 32, :] = zero_rows
    loads[0].wait()
    cols[...] = mm(select, tile[:, 1:9, 16:48, :].reshape(1024, 256)).astype(BF)
    pl.semaphore_wait(barrier, count)
    halo = halo_copies(tile, cols, left, right, hs, hr)
    for i in (2, 3, 4, 5, 6, 7, 0, 1):
        pl.when(halo[i][0])(halo[i][1].start)
    for t in range(4):
        for r in middle:
            xc[1, t, r * 32:r * 32 + 32, :] = tile[t, r, 16:48, :]

    def x_copy(i):
        ref = (lambda b: (b.at[1, :, 32:288], b.at[0, :, 32:288], b.at[2, :, 32:288], b.at[:, :, 0:32], b.at[:, :, 288:320])[i])
        return pltpu.make_async_remote_copy(
            src_ref=ref(xc), dst_ref=ref(xc2), send_sem=xcs, recv_sem=xcr, device_id=other, device_id_type=MESH)

    loads[1].wait()

    def forward(t, columns):
        total = None
        for f, a in FOLD[t]:
            for b in range(3):
                for c in columns:
                    lanes = slice(c * 256, c * 256 + 256)
                    weight = w_ref[a * 3 + b, lanes] if a < 3 else wsum[(a - 3) * 3 + b, lanes]
                    term = mm(xc[c, f, b * 32:b * 32 + 256, :], weight)
                    total = term if total is None else total + term
        return total

    for t in (3, 2):
        acc_ref[t] = forward(t, (1,))
    for b in range(3):
        two = w_ref[b].astype(F32) + w_ref[3 + b].astype(F32)
        wsum[b] = two.astype(BF)
        wsum[3 + b] = (two + w_ref[6 + b].astype(F32)).astype(BF)
    for t in (1, 0):
        acc_ref[t] = forward(t, (1,))
    halo_wait(tile, left, right, hr, (2, 3))
    shifted(tile, left, right, xc, middle, False)
    for i in range(3):
        x_copy(i).start()
    for t in range(4):
        acc_ref[t] += forward(t, (0, 2))
    halo_wait(tile, left, right, hr, (0, 1, 4, 5, 6, 7))
    shifted(tile, left, right, xc, ends, True)
    x_copy(3).start()
    x_copy(4).start()
    for side, (lo, b) in enumerate(((0, 0), (288, 2))):
        total = None
        for a in range(3):
            for c in range(3):
                rows = jnp.concatenate([xc[c, max(t + a - 2, 0), lo:lo + 32, :] for t in range(4)], axis=0)
                term = mm(rows, w_ref[a * 3 + b, c * 256:c * 256 + 256])
                total = term if total is None else total + term
        fix_ref[side] = total
    loads[2].wait()

    def g_copy(t):
        return pltpu.make_async_remote_copy(
            src_ref=gt.at[:, 1 - core, :, t * 256:t * 256 + 256], dst_ref=gt2.at[:, :, t * 256:t * 256 + 256],
            send_sem=gts, recv_sem=gtr, device_id=other, device_id_type=MESH)

    for t in range(4):
        acc_ref[t, 0:32] += fix_ref[0, t * 32:t * 32 + 32]
        acc_ref[t, 224:256] += fix_ref[1, t * 32:t * 32 + 32]
        acc = acc_ref[t]
        logistic = jax.nn.sigmoid(acc)
        grad = cot[t].reshape(256, 256).astype(F32) * logistic * (1.0 + acc * (1.0 - logistic))
        grad = grad.astype(BF)
        gtile[t, 1:9, 16:48, :] = grad.reshape(8, 32, 256)
        gt[:, :, :, t * 256:t * 256 + 256] = grad.T.reshape(8, 2, 16, 256)
        g_copy(t).start()

    low = iota((128, 128), 1) < 64

    def tap_term(tap, both):
        a, b, c = tap // 9, (tap // 3) % 3, tap % 3
        total = None
        for mine in both:
            for t in range(4):
                lanes = slice(t * 256, t * 256 + 256)
                one = gt[:, core, :, lanes] if mine else gt2[:, :, lanes]
                window = (xc if mine else xc2)[c, max(t + a - 2, 0), b * 32:b * 32 + 256, :]
                term = mm(one.reshape(128, 256), window)
                total = term if total is None else total + term
        return total

    def store_pair(p, by_y):
        for half in range(2):
            lanes = slice(half * 128, half * 128 + 128)
            one, two = hold[p % 4, 0, :, lanes], hold[p % 4, 1, :, lanes]
            both = (jnp.where(low, one, pltpu.roll(two, 64, 1)), jnp.where(low, pltpu.roll(one, 64, 1), two))
            for k, block in enumerate(both):
                for zz in range(2):
                    for yy in range(4):
                        rows = block[(zz * 4 + yy) * 16:(zz * 4 + yy) * 16 + 16]
                        i, j = (yy, 2 * half + k) if by_y else (2 * half + k, yy)
                        part[p, i, j, zz * 16:zz * 16 + 16] = rows
                        partb[p, i, j, zz * 16:zz * 16 + 16] = rows.astype(BF)

    def arrived(ref, sem):
        pltpu.make_async_copy(ref, ref, sem).wait()

    def first_copy(p, d, by_y):
        return pltpu.make_async_remote_copy(
            src_ref=partb.at[p, ((y if by_y else x) + d) % 4], dst_ref=r1.at[p, d - 1],
            send_sem=s1s, recv_sem=s1r.at[p // 4],
            device_id=device(dy=d) if by_y else device(dx=d), device_id_type=MESH)

    def second_copy(p, d, by_y, q):
        return pltpu.make_async_remote_copy(
            src_ref=s1b.at[p, ((y if by_y else x) + d) % 4], dst_ref=r2.at[p, d - 1],
            send_sem=s2s, recv_sem=s2r.at[q],
            device_id=device(dy=d) if by_y else device(dx=d), device_id_type=MESH)

    def third_copy(q, d):
        nz = (z + d) % 8
        return pltpu.make_async_remote_copy(
            src_ref=ob.at[nz % 4, nz // 4, q], dst_ref=r3.at[q, d - 1], send_sem=s3s, recv_sem=s3r.at[q],
            device_id=device(dz=d), device_id_type=MESH)

    def over_pairs(q, body):
        @pl.loop(2 * q, min(2 * q + 2, PAIRS // 2))
        def _(i):
            for k in range(2):
                body(2 * i + k, k == 0)

    def own_terms(pairs):
        for p in pairs:
            for i in range(2):
                hold[p, i] = tap_term(2 * p + i, (True,))

    def pair_terms(p):
        for i in range(2):
            tap = min(2 * p + i, 26)
            hold[p % 4, i] = hold[p, i] + tap_term(tap, (False,)) if p < 4 else tap_term(tap, (True, False))

    def weight_group(done, new):
        for p in new:
            pair_terms(p)
        for p in done:
            store_pair(p, p % 2 == 0)
        for p in done:
            for d in (1, 3, 2):
                first_copy(p, d, p % 2 == 0).start()

    def first_sum(q):
        def body(p, by_y):
            total = part[p, y if by_y else x]
            for d in range(3):
                total = total + r1[p, d].astype(F32)
            s1[p] = total
            s1b[p] = total.astype(BF)
            for d in (1, 3, 2):
                second_copy(p, d, not by_y, q).start()
        arrived(r1.at[4 * q:min(4 * q + 4, PAIRS)], s1r.at[q])
        over_pairs(q, body)

    lane = iota((32, 128), 1)

    def exchange(one, two, width):
        lower = (lane // width) % 2 == 0
        return (jnp.where(lower, one, pltpu.roll(two, width, 1)),
                jnp.where(lower, pltpu.roll(one, 128 - width, 1), two))

    def second_sum(q):
        def body(p, by_y):
            total = s1[p, x if by_y else y]
            for d in range(3):
                total = total + r2[p, d].astype(F32)
            s2[p] = total
        arrived(r2.at[4 * q:min(4 * q + 4, PAIRS)], s2r.at[q])
        over_pairs(q, body)
        v = [s2[4 * q + i] if 4 * q + i < PAIRS else jnp.zeros((32, 128), F32) for i in range(4)]
        v[0], v[1] = exchange(v[0], v[1], 16)
        v[2], v[3] = exchange(v[2], v[3], 16)
        v[0], v[2] = exchange(v[0], v[2], 32)
        v[1], v[3] = exchange(v[1], v[3], 32)
        for i in range(4):
            for zz in range(2):
                of[i, zz, q] = v[i][zz * 16:zz * 16 + 16]
                ob[i, zz, q] = v[i][zz * 16:zz * 16 + 16].astype(BF)
        for d in (4, 3, 5, 2, 6, 1, 7):
            third_copy(q, d).start()

    def feature_gradient(t):
        terms = [(t + 2 - a, a) for a in range(3) if t + 2 - a < 4] if t else [(2, 0), (1, 3), (0, 4)]
        total = None
        for f, a in terms:
            for b in range(3):
                for c in range(3):
                    index = a * 3 + 2 - b if a < 3 else (a - 3) * 3 + 2 - b
                    weight = (w_ref if a < 3 else wsum)[index, (2 - c) * 256:(2 - c) * 256 + 256, :]
                    term = nt(xg[c, f, b * 32:b * 32 + 256, :], weight)
                    total = term if total is None else total + term
        total = total + cot[t].reshape(256, 256).astype(F32)
        fg[t] = total.astype(BF).reshape(8, 32, 256)

    for present, copy in halo:
        pl.when(present)(copy.wait_send)
    ghalo = halo_copies(gtile, gcols, gleft, gright, hs, ghr)
    for i in (0, 1):
        pl.when(ghalo[i][0])(ghalo[i][1].start)
    own_terms(range(4))
    arrived(gt2, gtr)
    arrived(xc2, xcr)
    weight_group((), (0,))
    weight_group((0,), ())
    weight_group((), (1,))
    weight_group((1,), (2, 3))
    gcols[...] = mm(select, gtile[:, 1:9, 16:48, :].reshape(1024, 256)).astype(BF)
    for i in range(2, 8):
        pl.when(ghalo[i][0])(ghalo[i][1].start)
    weight_group((2, 3), (4, 5))
    weight_group((4, 5), (6, 7))
    weight_group((6, 7), (8, 9))
    weight_group((8, 9), (10, 11))
    weight_group((10, 11), (12, 13))
    weight_group((12, 13), ())
    halo_wait(gtile, gleft, gright, ghr, range(8))
    shifted(gtile, gleft, gright, xg, tuple(range(10)), True)
    feature_gradient(3)
    feature_gradient(2)
    for q in range(4):
        first_sum(q)
    second_sum(0)
    second_sum(1)
    feature_gradient(1)
    second_sum(2)
    second_sum(3)
    for t in range(4):
        acc = acc_ref[t]
        own = tile[t, 1:9, 16:48, :].reshape(256, 256).astype(F32)
        bo[t] = (own + acc * jax.nn.sigmoid(acc)).astype(BF).reshape(8, 32, 256)
    bo_out = pltpu.make_async_copy(bo, bo_hbm, local_sem.at[0])
    bo_out.start()
    feature_gradient(0)
    fg_out = pltpu.make_async_copy(fg, fg_hbm, local_sem.at[1])
    fg_out.start()
    for q in range(4):
        arrived(r3.at[q], s3r.at[q])
        total = of[zlo, zhi, q]
        for d in range(7):
            total = total + r3[q, d].astype(F32)
        wg_ref[q] = total * (1.0 / 512.0)

    for present, copy in ghalo:
        pl.when(present)(copy.wait_send)
    arrived(xc, xcs)
    arrived(gt2, gts)
    arrived(r1, s1s)
    arrived(r2, s2s)
    arrived(r3, s3s)
    bo_out.wait()
    fg_out.wait()


def finish(bo_in, fg_in, packed, bo_out, fg_out, wg_out, flat, sems):
    copies = [pltpu.make_async_copy(bo_in, bo_out, sems.at[0]), pltpu.make_async_copy(fg_in, fg_out, sems.at[1])]
    for copy in copies:
        copy.start()
    for q in range(4):
        flipped = packed[q].T
        for e in range(8):
            tap = 8 * q + 2 * (e % 4) + e // 4
            flat[tap * 16:tap * 16 + 16, :] = flipped[e * 16:e * 16 + 16, :]
    for k in range(16):
        wg_out[k] = flat[pl.ds(k, 32, stride=16), :].T[:, :27]
    for copy in copies:
        copy.wait()


def per_device(features, weights, cotangent):
    dma = pltpu.SemaphoreType.DMA
    anywhere = pl.BlockSpec(memory_space=pl.ANY)
    vmem = pl.BlockSpec(memory_space=pltpu.VMEM)
    block = jax.ShapeDtypeStruct((4, 8, 32, 256), BF)
    block_out, feature_grad, packed = pl.pallas_call(
        kernel,
        out_shape=(block, block, jax.ShapeDtypeStruct((4, 16, 128), F32)),
        in_specs=[anywhere] * 3,
        out_specs=(anywhere, anywhere, vmem),
        scratch_shapes=[
            pltpu.VMEM((9, 768, 256), BF), pltpu.VMEM((6, 768, 256), BF),
            pltpu.VMEM((4, 10, 64, 256), BF), pltpu.VMEM((4, 10, 64, 256), BF),
            pltpu.VMEM((3, 4, 320, 256), BF), pltpu.VMEM((3, 4, 320, 256), BF), pltpu.VMEM((3, 4, 320, 256), BF),
            pltpu.VMEM((4, 8, 32, 256), BF), pltpu.VMEM((4, 8, 32, 256), BF), pltpu.VMEM((4, 8, 32, 256), BF),
            pltpu.VMEM((4, 256, 256), F32), pltpu.VMEM((2, 128, 256), F32), pltpu.VMEM((4, 2, 128, 256), F32),
            pltpu.VMEM((8, 2, 16, 1024), BF), pltpu.VMEM((8, 16, 1024), BF),
            pltpu.VMEM((128, 256), BF), pltpu.VMEM((128, 256), BF),
            pltpu.VMEM((64, 256), BF), pltpu.VMEM((64, 256), BF), pltpu.VMEM((64, 256), BF), pltpu.VMEM((64, 256), BF),
            pltpu.VMEM((PAIRS, 4, 4, 32, 128), F32), pltpu.VMEM((PAIRS, 4, 4, 32, 128), BF),
            pltpu.VMEM((PAIRS, 3, 4, 32, 128), BF),
            pltpu.VMEM((PAIRS, 4, 32, 128), F32), pltpu.VMEM((PAIRS, 4, 32, 128), BF),
            pltpu.VMEM((PAIRS, 3, 32, 128), BF), pltpu.VMEM((PAIRS, 32, 128), F32),
            pltpu.VMEM((4, 2, 4, 16, 128), F32), pltpu.VMEM((4, 2, 4, 16, 128), BF), pltpu.VMEM((4, 7, 16, 128), BF),
            dma((3,)), dma((8,)), dma((8,)), dma((8,)), dma, dma, dma, dma,
            dma, dma((4,)), dma, dma((4,)), dma, dma((4,)),
        ],
        compiler_params=pltpu.CompilerParams(collective_id=0, has_side_effects=True, vmem_limit_bytes=60 << 20),
        cost_estimate=pl.CostEstimate(flops=9_000_000_000, bytes_accessed=6_000_000, transcendentals=300_000),
        name="conv_block",
    )(features, weights.reshape(9, 768, 256), cotangent)
    block_out, feature_grad, grads = pl.pallas_call(
        finish,
        out_shape=(block, block, jax.ShapeDtypeStruct((16, 16, 27), F32)),
        in_specs=[vmem] * 3,
        out_specs=(anywhere, anywhere, vmem),
        scratch_shapes=[pltpu.VMEM((512, 16), F32), dma((2,))],
        name="finish",
    )(block_out, feature_grad, packed)
    return block_out, feature_grad, grads.transpose(2, 0, 1)


def solution(mesh):
    in_specs = (P(None, "ha", "wa", None), P(), P(None, "ha", "wa", None))
    out_specs = (P(None, "ha", "wa", None), P(None, "ha", "wa", None), P(None, "ha", "wa"))
    return jax.shard_map(
        per_device, mesh=mesh, in_specs=in_specs, out_specs=out_specs, check_vma=False
    )
```

```python
import jax
import jax.numpy as jnp
from jax import lax
from jax.experimental import pallas as pl
from jax.experimental.pallas import tpu as pltpu
from jax.sharding import PartitionSpec as P

MESH = pl.DeviceIdType.MESH
BF, F32 = jnp.bfloat16, jnp.float32
PAIRS = 14
FOLD = (((0, 4),), ((0, 3), (1, 2)), ((0, 0), (1, 1), (2, 2)), ((1, 0), (2, 1), (3, 2)))


def mm(a, b):
    return jnp.dot(a, b, preferred_element_type=F32)


def nt(a, b):
    return lax.dot_general(a, b, (((1,), (1,)), ((), ())), preferred_element_type=F32)


def iota(shape, dim):
    return lax.broadcasted_iota(jnp.int32, shape, dim)


def kernel(
    feat_hbm, w_hbm, cot_hbm,
    bo_hbm, fg_hbm, wg_ref,
    w_ref, wsum, tile, gtile, xc, xc2, xg, cot, bo, fg, acc_ref, fix_ref, hold, gt, gt2,
    cols, gcols, left, right, gleft, gright,
    part, partb, r1, s1, s1b, r2, s2, of, ob, r3,
    local_sem, hs, hr, ghr, xcs, xcr, gts, gtr, s1s, s1r, s2s, s2r, s3s, s3r,
):
    ha, wa = lax.axis_index("ha"), lax.axis_index("wa")
    x, zlo = ha // 4, ha % 4
    zhi, y, core = wa // 8, (wa // 2) % 4, wa % 2
    z = zhi * 4 + zlo

    def device(dx=0, dy=0, dz=0, dc=0):
        nx, ny, nz, nc = (x + dx) % 4, (y + dy) % 4, (z + dz) % 8, (core + dc) % 2
        return (nx * 4 + nz % 4, (nz // 4) * 8 + ny * 2 + nc)

    other = device(dc=1)
    north, south, west, east = ha > 0, ha < 15, wa > 0, wa < 15
    sides = (
        (north, -1, 0), (south, 1, 0), (west, 0, -1), (east, 0, 1),
        (north & west, -1, -1), (north & east, -1, 1), (south & west, 1, -1), (south & east, 1, 1),
    )

    loads = [
        pltpu.make_async_copy(feat_hbm, tile.at[:, 1:9, 16:48, :], local_sem.at[0]),
        pltpu.make_async_copy(w_hbm, w_ref, local_sem.at[1]),
        pltpu.make_async_copy(cot_hbm, cot, local_sem.at[2]),
    ]
    for copy in loads:
        copy.start()

    barrier = pltpu.get_barrier_semaphore()
    count = 14
    for present, dr, dc in sides:
        @pl.when(present)
        def _():
            pl.semaphore_signal(barrier, inc=1, device_id=(ha + dr, wa + dc), device_id_type=MESH)
        count = count + present.astype(jnp.int32)
    peers = [device(dy=d) for d in (1, 2, 3)] + [device(dx=d) for d in (1, 2, 3)]
    peers += [device(dz=d) for d in range(1, 8)] + [other]
    for peer in peers:
        pl.semaphore_signal(barrier, inc=1, device_id=peer, device_id_type=MESH)

    m, n = iota((128, 1024), 0), iota((128, 1024), 1)
    column = jnp.where(m < 64, 31, 0)
    place = m % 64
    pick = jnp.where(place < 32, place * 32, jnp.where(place < 48, (place - 32) * 256, (place - 48) * 256 + 224)) + column
    select = jnp.where(pick == n, 1.0, 0.0).astype(BF)
    m, n = iota((512, 32), 0), iota((512, 32), 1)
    spread = jnp.where(m // 16 == n, 1.0, 0.0).astype(BF)
    m, n = iota((128, 32), 0), iota((128, 32), 1)
    corner = jnp.where(m // 64 * 16 + (m % 64) // 16 == n, 1.0, 0.0).astype(BF)

    def halo_copies(padded, packed, lhs, rhs, send, recv):
        row_src = {-1: padded.at[:, 1, 16:48, :], 1: padded.at[:, 8, 16:48, :]}
        row_dst = {-1: padded.at[:, 9, 16:48, :], 1: padded.at[:, 0, 16:48, :]}
        copies = []
        for i, (present, dr, dc) in enumerate(sides):
            if dc == 0:
                src, dst = row_src[dr], row_dst[dr]
            else:
                base = 0 if dc == 1 else 64
                target = lhs if dc == 1 else rhs
                if dr == 0:
                    src, dst = packed.at[base:base + 32], target.at[0:32]
                elif dr == -1:
                    src, dst = packed.at[base + 32:base + 48], target.at[48:64]
                else:
                    src, dst = packed.at[base + 48:base + 64], target.at[32:48]
            back = {(-1, 0): 1, (1, 0): 0, (0, -1): 3, (0, 1): 2, (-1, -1): 7, (-1, 1): 6, (1, -1): 5, (1, 1): 4}[(dr, dc)]
            copies.append((present, pltpu.make_async_remote_copy(
                src_ref=src, dst_ref=dst, send_sem=send.at[i], recv_sem=recv.at[back],
                device_id=(ha + dr, wa + dc), device_id_type=MESH)))
        return copies

    def halo_wait(padded, lhs, rhs, recv, which):
        landing = (
            padded.at[:, 0, 16:48, :], padded.at[:, 9, 16:48, :], lhs.at[0:32], rhs.at[0:32],
            lhs.at[32:48], rhs.at[32:48], lhs.at[48:64], rhs.at[48:64],
        )
        for i in which:
            present, ref = sides[i][0], landing[i]

            @pl.when(present)
            def _():
                pltpu.make_async_copy(ref, ref, recv.at[i]).wait()

            @pl.when(jnp.logical_not(present))
            def _():
                ref[...] = jnp.zeros(ref.shape, BF)

    def shifted(padded, lhs, rhs, out, rows, centre):
        if 1 in rows:
            padded[:, 1:9, 0:16, :] = mm(spread, lhs[0:32]).astype(BF).reshape(4, 8, 16, 256)
            padded[:, 1:9, 48:64, :] = mm(spread, rhs[0:32]).astype(BF).reshape(4, 8, 16, 256)
        if 0 in rows:
            for side, lanes in ((lhs, slice(0, 16)), (rhs, slice(48, 64))):
                ends = mm(corner, side[32:64]).astype(BF).reshape(2, 4, 16, 256)
                padded[:, 0, lanes, :] = ends[0]
                padded[:, 9, lanes, :] = ends[1]
        for t in range(4):
            for r in rows:
                for c in range(3):
                    if c != 1 or centre:
                        out[c, t, r * 32:r * 32 + 32, :] = padded[t, r, 15 + c:47 + c, :]

    middle, ends = tuple(range(1, 9)), (0, 9)

    zero_rows = jnp.zeros((32, 256), BF)
    for c in range(3):
        for t in range(4):
            for r in ends:
                xc[c, t, r * 32:r * 32 + 32, :] = zero_rows
    loads[0].wait()
    cols[...] = mm(select, tile[:, 1:9, 16:48, :].reshape(1024, 256)).astype(BF)
    pl.semaphore_wait(barrier, count)
    halo = halo_copies(tile, cols, left, right, hs, hr)
    for i in (2, 3, 0, 1, 4, 5, 6, 7):
        pl.when(halo[i][0])(halo[i][1].start)
    for t in range(4):
        for r in middle:
            xc[1, t, r * 32:r * 32 + 32, :] = tile[t, r, 16:48, :]

    def x_copy(i):
        ref = (lambda b: (b.at[1, :, 32:288], b.at[0, :, 32:288], b.at[2, :, 32:288], b.at[:, :, 0:32], b.at[:, :, 288:320])[i])
        return pltpu.make_async_remote_copy(
            src_ref=ref(xc), dst_ref=ref(xc2), send_sem=xcs, recv_sem=xcr, device_id=other, device_id_type=MESH)

    loads[1].wait()

    def forward(t, columns):
        total = None
        for f, a in FOLD[t]:
            for b in range(3):
                for c in columns:
                    lanes = slice(c * 256, c * 256 + 256)
                    weight = w_ref[a * 3 + b, lanes] if a < 3 else wsum[(a - 3) * 3 + b, lanes]
                    term = mm(xc[c, f, b * 32:b * 32 + 256, :], weight)
                    total = term if total is None else total + term
        return total

    for t in (3, 2):
        acc_ref[t] = forward(t, (1,))
    for b in range(3):
        two = w_ref[b].astype(F32) + w_ref[3 + b].astype(F32)
        wsum[b] = two.astype(BF)
        wsum[3 + b] = (two + w_ref[6 + b].astype(F32)).astype(BF)
    for t in (1, 0):
        acc_ref[t] = forward(t, (1,))
    halo_wait(tile, left, right, hr, (2, 3))
    shifted(tile, left, right, xc, middle, False)
    for i in range(3):
        x_copy(i).start()
    for t in range(4):
        acc_ref[t] += forward(t, (0, 2))
    halo_wait(tile, left, right, hr, (0, 1, 4, 5, 6, 7))
    shifted(tile, left, right, xc, ends, True)
    x_copy(3).start()
    x_copy(4).start()
    for side, (lo, b) in enumerate(((0, 0), (288, 2))):
        total = None
        for a in range(3):
            for c in range(3):
                rows = jnp.concatenate([xc[c, max(t + a - 2, 0), lo:lo + 32, :] for t in range(4)], axis=0)
                term = mm(rows, w_ref[a * 3 + b, c * 256:c * 256 + 256])
                total = term if total is None else total + term
        fix_ref[side] = total
    loads[2].wait()

    def g_copy(t):
        return pltpu.make_async_remote_copy(
            src_ref=gt.at[:, 1 - core, :, t * 256:t * 256 + 256], dst_ref=gt2.at[:, :, t * 256:t * 256 + 256],
            send_sem=gts, recv_sem=gtr, device_id=other, device_id_type=MESH)

    for t in range(4):
        acc_ref[t, 0:32] += fix_ref[0, t * 32:t * 32 + 32]
        acc_ref[t, 224:256] += fix_ref[1, t * 32:t * 32 + 32]
        acc = acc_ref[t]
        logistic = jax.nn.sigmoid(acc)
        own = tile[t, 1:9, 16:48, :].reshape(256, 256).astype(F32)
        bo[t] = (own + acc * logistic).astype(BF).reshape(8, 32, 256)
        grad = cot[t].reshape(256, 256).astype(F32) * logistic * (1.0 + acc * (1.0 - logistic))
        grad = grad.astype(BF)
        gtile[t, 1:9, 16:48, :] = grad.reshape(8, 32, 256)
        gt[:, :, :, t * 256:t * 256 + 256] = grad.T.reshape(8, 2, 16, 256)
        g_copy(t).start()

    low = iota((128, 128), 1) < 64

    def tap_term(tap, both):
        a, b, c = tap // 9, (tap // 3) % 3, tap % 3
        total = None
        for mine in both:
            for t in range(4):
                lanes = slice(t * 256, t * 256 + 256)
                one = gt[:, core, :, lanes] if mine else gt2[:, :, lanes]
                window = (xc if mine else xc2)[c, max(t + a - 2, 0), b * 32:b * 32 + 256, :]
                term = mm(one.reshape(128, 256), window)
                total = term if total is None else total + term
        return total

    def store_pair(p, by_y):
        for half in range(2):
            lanes = slice(half * 128, half * 128 + 128)
            one, two = hold[p % 4, 0, :, lanes], hold[p % 4, 1, :, lanes]
            both = (jnp.where(low, one, pltpu.roll(two, 64, 1)), jnp.where(low, pltpu.roll(one, 64, 1), two))
            for k, block in enumerate(both):
                for zz in range(2):
                    for yy in range(4):
                        rows = block[(zz * 4 + yy) * 16:(zz * 4 + yy) * 16 + 16]
                        i, j = (yy, 2 * half + k) if by_y else (2 * half + k, yy)
                        part[p, i, j, zz * 16:zz * 16 + 16] = rows
                        partb[p, i, j, zz * 16:zz * 16 + 16] = rows.astype(BF)

    def arrived(ref, sem):
        pltpu.make_async_copy(ref, ref, sem).wait()

    def first_copy(p, d, by_y):
        return pltpu.make_async_remote_copy(
            src_ref=partb.at[p, ((y if by_y else x) + d) % 4], dst_ref=r1.at[p, d - 1],
            send_sem=s1s, recv_sem=s1r.at[p // 4],
            device_id=device(dy=d) if by_y else device(dx=d), device_id_type=MESH)

    def second_copy(p, d, by_y, q):
        return pltpu.make_async_remote_copy(
            src_ref=s1b.at[p, ((y if by_y else x) + d) % 4], dst_ref=r2.at[p, d - 1],
            send_sem=s2s, recv_sem=s2r.at[q],
            device_id=device(dy=d) if by_y else device(dx=d), device_id_type=MESH)

    def third_copy(q, d):
        nz = (z + d) % 8
        return pltpu.make_async_remote_copy(
            src_ref=ob.at[nz % 4, nz // 4, q], dst_ref=r3.at[q, d - 1], send_sem=s3s, recv_sem=s3r.at[q],
            device_id=device(dz=d), device_id_type=MESH)

    def over_pairs(q, body):
        @pl.loop(2 * q, min(2 * q + 2, PAIRS // 2))
        def _(i):
            for k in range(2):
                body(2 * i + k, k == 0)

    def own_terms(pairs):
        for p in pairs:
            for i in range(2):
                hold[p, i] = tap_term(2 * p + i, (True,))

    def pair_terms(p):
        for i in range(2):
            tap = min(2 * p + i, 26)
            hold[p % 4, i] = hold[p, i] + tap_term(tap, (False,)) if p < 4 else tap_term(tap, (True, False))

    def weight_group(done, new):
        for p in new:
            pair_terms(p)
        for p in done:
            store_pair(p, p % 2 == 0)
        for p in done:
            for d in (1, 3, 2):
                first_copy(p, d, p % 2 == 0).start()

    def first_sum(q):
        def body(p, by_y):
            total = part[p, y if by_y else x]
            for d in range(3):
                total = total + r1[p, d].astype(F32)
            s1[p] = total
            s1b[p] = total.astype(BF)
            for d in (1, 3, 2):
                second_copy(p, d, not by_y, q).start()
        arrived(r1.at[4 * q:min(4 * q + 4, PAIRS)], s1r.at[q])
        over_pairs(q, body)

    lane = iota((32, 128), 1)

    def exchange(one, two, width):
        lower = (lane // width) % 2 == 0
        return (jnp.where(lower, one, pltpu.roll(two, width, 1)),
                jnp.where(lower, pltpu.roll(one, 128 - width, 1), two))

    def second_sum(q):
        def body(p, by_y):
            total = s1[p, x if by_y else y]
            for d in range(3):
                total = total + r2[p, d].astype(F32)
            s2[p] = total
        arrived(r2.at[4 * q:min(4 * q + 4, PAIRS)], s2r.at[q])
        over_pairs(q, body)
        v = [s2[4 * q + i] if 4 * q + i < PAIRS else jnp.zeros((32, 128), F32) for i in range(4)]
        v[0], v[1] = exchange(v[0], v[1], 16)
        v[2], v[3] = exchange(v[2], v[3], 16)
        v[0], v[2] = exchange(v[0], v[2], 32)
        v[1], v[3] = exchange(v[1], v[3], 32)
        for i in range(4):
            for zz in range(2):
                of[i, zz, q] = v[i][zz * 16:zz * 16 + 16]
                ob[i, zz, q] = v[i][zz * 16:zz * 16 + 16].astype(BF)
        for d in (4, 3, 5, 2, 6, 1, 7):
            third_copy(q, d).start()

    def feature_gradient(t):
        terms = [(t + 2 - a, a) for a in range(3) if t + 2 - a < 4] if t else [(2, 0), (1, 3), (0, 4)]
        total = None
        for f, a in terms:
            for b in range(3):
                for c in range(3):
                    index = a * 3 + 2 - b if a < 3 else (a - 3) * 3 + 2 - b
                    weight = (w_ref if a < 3 else wsum)[index, (2 - c) * 256:(2 - c) * 256 + 256, :]
                    term = nt(xg[c, f, b * 32:b * 32 + 256, :], weight)
                    total = term if total is None else total + term
        total = total + cot[t].reshape(256, 256).astype(F32)
        fg[t] = total.astype(BF).reshape(8, 32, 256)

    for present, copy in halo:
        pl.when(present)(copy.wait_send)
    ghalo = halo_copies(gtile, gcols, gleft, gright, hs, ghr)
    for i in (0, 1):
        pl.when(ghalo[i][0])(ghalo[i][1].start)
    own_terms(range(4))
    arrived(gt2, gtr)
    arrived(xc2, xcr)
    weight_group((), (0,))
    weight_group((0,), (1,))
    weight_group((1,), (2, 3))
    gcols[...] = mm(select, gtile[:, 1:9, 16:48, :].reshape(1024, 256)).astype(BF)
    for i in range(2, 8):
        pl.when(ghalo[i][0])(ghalo[i][1].start)
    weight_group((2, 3), (4, 5))
    weight_group((4, 5), (6, 7))
    weight_group((6, 7), (8, 9))
    weight_group((8, 9), (10, 11))
    bo_out = pltpu.make_async_copy(bo, bo_hbm, local_sem.at[0])
    bo_out.start()
    weight_group((10, 11), (12, 13))
    weight_group((12, 13), ())
    halo_wait(gtile, gleft, gright, ghr, range(8))
    shifted(gtile, gleft, gright, xg, tuple(range(10)), True)
    feature_gradient(3)
    feature_gradient(2)
    for q in range(4):
        first_sum(q)
    second_sum(0)
    second_sum(1)
    feature_gradient(1)
    second_sum(2)
    second_sum(3)
    feature_gradient(0)
    fg_out = pltpu.make_async_copy(fg, fg_hbm, local_sem.at[1])
    fg_out.start()
    for q in range(4):
        arrived(r3.at[q], s3r.at[q])
        total = of[zlo, zhi, q]
        for d in range(7):
            total = total + r3[q, d].astype(F32)
        wg_ref[q] = total * (1.0 / 512.0)

    for present, copy in ghalo:
        pl.when(present)(copy.wait_send)
    arrived(xc, xcs)
    arrived(gt2, gts)
    arrived(r1, s1s)
    arrived(r2, s2s)
    arrived(r3, s3s)
    bo_out.wait()
    fg_out.wait()


def finish(bo_in, fg_in, packed, bo_out, fg_out, wg_out, flat, held, sems):
    loads, copies = [], []
    for i, (src, dst) in enumerate(((bo_in, bo_out), (fg_in, fg_out))):
        for t in range(4):
            loads.append(pltpu.make_async_copy(src.at[t], held.at[i, t], sems.at[0, i, t]))
            copies.append(pltpu.make_async_copy(held.at[i, t], dst.at[t], sems.at[1, i, t]))
    for load in loads:
        load.start()
    for load, copy in zip(loads, copies):
        load.wait()
        copy.start()
    for q in range(4):
        flipped = packed[q].T
        for e in range(8):
            tap = 8 * q + 2 * (e % 4) + e // 4
            flat[tap * 16:tap * 16 + 16, :] = flipped[e * 16:e * 16 + 16, :]
    for k in range(16):
        wg_out[k] = flat[pl.ds(k, 32, stride=16), :].T[:, :27]
    for copy in copies:
        copy.wait()


def per_device(features, weights, cotangent):
    dma = pltpu.SemaphoreType.DMA
    anywhere = pl.BlockSpec(memory_space=pl.ANY)
    vmem = pl.BlockSpec(memory_space=pltpu.VMEM)
    block = jax.ShapeDtypeStruct((4, 8, 32, 256), BF)
    block_out, feature_grad, packed = pl.pallas_call(
        kernel,
        out_shape=(block, block, jax.ShapeDtypeStruct((4, 16, 128), F32)),
        in_specs=[anywhere] * 3,
        out_specs=(anywhere, anywhere, vmem),
        scratch_shapes=[
            pltpu.VMEM((9, 768, 256), BF), pltpu.VMEM((6, 768, 256), BF),
            pltpu.VMEM((4, 10, 64, 256), BF), pltpu.VMEM((4, 10, 64, 256), BF),
            pltpu.VMEM((3, 4, 320, 256), BF), pltpu.VMEM((3, 4, 320, 256), BF), pltpu.VMEM((3, 4, 320, 256), BF),
            pltpu.VMEM((4, 8, 32, 256), BF), pltpu.VMEM((4, 8, 32, 256), BF), pltpu.VMEM((4, 8, 32, 256), BF),
            pltpu.VMEM((4, 256, 256), F32), pltpu.VMEM((2, 128, 256), F32), pltpu.VMEM((4, 2, 128, 256), F32),
            pltpu.VMEM((8, 2, 16, 1024), BF), pltpu.VMEM((8, 16, 1024), BF),
            pltpu.VMEM((128, 256), BF), pltpu.VMEM((128, 256), BF),
            pltpu.VMEM((64, 256), BF), pltpu.VMEM((64, 256), BF), pltpu.VMEM((64, 256), BF), pltpu.VMEM((64, 256), BF),
            pltpu.VMEM((PAIRS, 4, 4, 32, 128), F32), pltpu.VMEM((PAIRS, 4, 4, 32, 128), BF),
            pltpu.VMEM((PAIRS, 3, 4, 32, 128), BF),
            pltpu.VMEM((PAIRS, 4, 32, 128), F32), pltpu.VMEM((PAIRS, 4, 32, 128), BF),
            pltpu.VMEM((PAIRS, 3, 32, 128), BF), pltpu.VMEM((PAIRS, 32, 128), F32),
            pltpu.VMEM((4, 2, 4, 16, 128), F32), pltpu.VMEM((4, 2, 4, 16, 128), BF), pltpu.VMEM((4, 7, 16, 128), BF),
            dma((3,)), dma((8,)), dma((8,)), dma((8,)), dma, dma, dma, dma,
            dma, dma((4,)), dma, dma((4,)), dma, dma((4,)),
        ],
        compiler_params=pltpu.CompilerParams(collective_id=0, has_side_effects=True, vmem_limit_bytes=60 << 20),
        cost_estimate=pl.CostEstimate(flops=9_000_000_000, bytes_accessed=6_000_000, transcendentals=300_000),
        name="conv_block",
    )(features, weights.reshape(9, 768, 256), cotangent)
    block_out, feature_grad, grads = pl.pallas_call(
        finish,
        out_shape=(block, block, jax.ShapeDtypeStruct((16, 16, 27), F32)),
        in_specs=[anywhere, anywhere, vmem],
        out_specs=(anywhere, anywhere, vmem),
        scratch_shapes=[pltpu.VMEM((512, 16), F32), pltpu.VMEM((2, 4, 8, 32, 256), BF), dma((2, 2, 4))],
        name="finish",
    )(block_out, feature_grad, packed)
    return block_out, feature_grad, grads.transpose(2, 0, 1)


def solution(mesh):
    in_specs = (P(None, "ha", "wa", None), P(), P(None, "ha", "wa", None))
    out_specs = (P(None, "ha", "wa", None), P(None, "ha", "wa", None), P(None, "ha", "wa"))
    return jax.shard_map(
        per_device, mesh=mesh, in_specs=in_specs, out_specs=out_specs, check_vma=False
    )
```
